32 devices in a mesh: space: 8 (over y, x, core), chan: 4 (over z).
Axes of the slice: x: 2, y: 2, z: 4, core: 2. Of those that a mesh axis runs over, the one named last changes fastest.
Arguments:
- volume: bfloat16 [32, 16, 8, 128], P(None, 'space', 'chan'), may hold values from -6 to 6
- weight_first: bfloat16 [3, 3, 3, 64, 32], replicated, may hold values from -0.21875 to 0.21875
- weight_deep: bfloat16 [3, 3, 3, 512, 64], P(None, None, None, 'chan'), may hold values from -0.15625 to 0.15625
- cotangent: bfloat16 [512, 8, 256], P('chan', 'space'), may hold values from -6 to 6
Outputs:
- deep_out: bfloat16 [512, 8, 256], P('chan', 'space')
- grad_deep: float32 [3, 3, 3, 512, 64], P(None, None, None, 'chan')
The draws below stay inside these ranges and needn't reach their ends.
All inputs are finite; a program needn't handle non-finite values.
Results may differ from the reference program's by a relative error of at most 0.0051.
Values may be sent and summed in bfloat16 or wider, within the bound.
No kernel may reach another device: no remote copies, remote signals or barrier semaphores. Data moves between devices by JAX's collectives and lax.ppermute only.
A program may use at most 64 MiB of HBM per device.

```python
import jax
import jax.numpy as jnp
from jax import lax

CIN = 32
CMID = 64
COUT = 512
NZ = 128
NX = 16
NY = 8
MX = 8
MY = 4
MZ = 64


def steps_of(stream_key, dims, split, least, high):
    def one(axis_at, parts):
        draws = jax.random.uniform(jax.random.fold_in(jax.random.fold_in(stream_key, 6), axis_at), (parts,), jnp.float32, least / len(split), high / len(split))
        return jnp.repeat(jnp.exp(draws), dims[axis_at] // parts).reshape((-1,) + (1,) * (len(dims) - axis_at - 1))

    level = one(*split[0])
    for cut in split[1:]:
        level = level * one(*cut)
    return level


def gaussian(stream_key, shape, spread, bound, shards=(), kind=jnp.bfloat16):
    loudness = steps_of(stream_key, shape, shards, -0.22, 0.18) if shards else 1.0
    entries = jax.random.normal(stream_key, shape, jnp.float32) * spread * loudness
    return jnp.minimum(jnp.maximum(entries, -bound), bound).astype(kind)


def setup_inputs(seed: int = 0) -> dict:
    keys = jax.random.split(jax.random.key(seed), 5)
    return {
        "volume": gaussian(keys[0], (CIN, NX, NY, NZ), 1.0, 6.0, ((1, 8), (2, 4))),
        "weight_first": gaussian(keys[1], (3, 3, 3, CMID, CIN), (27 * CIN) ** -0.5, 0.21875),
        "weight_deep": gaussian(keys[2], (3, 3, 3, COUT, CMID), (27 * CMID) ** -0.5, 0.15625, ((3, 4),)),
        "cotangent": gaussian(keys[3], (COUT, MX, MY * MZ), 1.0, 6.0, ((0, 4), (1, 8))),
    }


def convolve(padded, weight, planes, rows, depth):
    total = jnp.zeros((weight.shape[3], planes, rows, depth), jnp.float32)
    for offset_x in range(3):
        for offset_y in range(3):
            for offset_z in range(3):
                window = padded[:, offset_x:offset_x + planes, offset_y:offset_y + rows, offset_z:offset_z + depth]
                total = total + jnp.einsum("oc,cxyz->oxyz", weight[offset_x, offset_y, offset_z].astype(jnp.float32), window.astype(jnp.float32))
    return total


def weight_terms(grad_pre, padded, planes, rows, depth):
    outer = []
    for offset_x in range(3):
        middle = []
        for offset_y in range(3):
            inner = []
            for offset_z in range(3):
                window = padded[:, offset_x:offset_x + planes, offset_y:offset_y + rows, offset_z:offset_z + depth]
                inner.append(jnp.einsum("oxyz,cxyz->oc", grad_pre.astype(jnp.float32), window.astype(jnp.float32)))
            middle.append(jnp.stack(inner))
        outer.append(jnp.stack(middle))
    return jnp.stack(outer)


def pool_mean(act):
    chans, planes, rows, depth = act.shape
    blocks = act.reshape(chans, planes // 2, 2, rows // 2, 2, depth // 2, 2)
    return jnp.mean(blocks, axis=(2, 4, 6))


def reference(volume, weight_first, weight_deep, cotangent):
    padded_in = jnp.pad(volume, ((0, 0), (1, 1), (1, 1), (1, 1)))

    def first_block(index):
        slab = lax.dynamic_slice_in_dim(padded_in, (index * 2).astype(jnp.int32), 4, axis=1)
        pre_first = convolve(slab, weight_first, 2, NY, NZ)
        return pool_mean(jax.nn.silu(pre_first)).astype(jnp.bfloat16)

    blocks = lax.map(first_block, jnp.arange(MX, dtype=jnp.int32))
    pooled = jnp.moveaxis(blocks[:, :, 0], 0, 1)
    padded_pool = jnp.pad(pooled, ((0, 0), (1, 1), (1, 1), (1, 1)))

    def deep_plane(grad, index):
        slab = lax.dynamic_slice_in_dim(padded_pool, index.astype(jnp.int32), 3, axis=1)
        pre_deep = convolve(slab, weight_deep, 1, MY, MZ)
        out = jax.nn.silu(pre_deep).astype(jnp.bfloat16)
        cot_flat = lax.dynamic_slice_in_dim(cotangent, index.astype(jnp.int32), 1, axis=1)
        cot = cot_flat.reshape(COUT, 1, MY, MZ).astype(jnp.float32)
        sigma = jax.nn.sigmoid(pre_deep)
        grad_pre = (cot * sigma * (1.0 + pre_deep * (1.0 - sigma))).astype(jnp.bfloat16)
        grad = grad + weight_terms(grad_pre, slab, 1, MY, MZ)
        return grad, out

    start = jnp.zeros((3, 3, 3, COUT, CMID), jnp.float32)
    grad_deep, outs = lax.scan(deep_plane, start, jnp.arange(MX, dtype=jnp.int32))
    deep_out = jnp.moveaxis(outs[:, :, 0], 0, 1).reshape(COUT, MX, MY * MZ)
    return deep_out, grad_deep
```

```python
import functools

import jax
import jax.numpy as jnp
from jax import lax
from jax.experimental import pallas as pl
from jax.experimental.pallas import tpu as pltpu
from jax.sharding import PartitionSpec as P


def padded_2(array, sides, width):
    for axis, dim in sides:
        peers, length = (lax.axis_size(axis), array.shape[dim])
        up = [(i, (i + 1) % peers) for i in range(peers - 1)]
        down = [(j, i) for i, j in up]
        last = lax.slice_in_dim(array, length - width, length, axis=dim)
        leading = lax.slice_in_dim(array, 0, width, axis=dim)
        before = lax.ppermute(last, axis, up)
        after = lax.ppermute(leading, axis, down)
        array = jnp.concatenate([before, array, after], axis=dim)
    return array


def windows(padded, planes, rows, depth):
    for offset_x in range(3):
        for offset_y in range(3):
            for offset_z in range(3):
                yield (offset_x, offset_y, offset_z), padded[
                    :,
                    offset_x : offset_x + planes,
                    offset_y : offset_y + rows,
                    offset_z : offset_z + depth,
                ]


def convolve(padded, weight, planes, rows, depth):
    total = jnp.zeros((weight.shape[3], planes, rows, depth), jnp.float32)
    for tap, window in windows(padded, planes, rows, depth):
        total = total + jnp.einsum(
            "oc,cxyz->oxyz", weight[tap], window, preferred_element_type=jnp.float32
        )
    return total


def weight_terms(grad_pre, padded, planes, rows, depth):
    terms = [
        jnp.einsum("oxyz,cxyz->oc", grad_pre, window, preferred_element_type=jnp.float32)
        for _, window in windows(padded, planes, rows, depth)
    ]
    return jnp.stack(terms).reshape((3, 3, 3) + terms[0].shape)


def pool_mean(act):
    chans, planes, rows, depth = act.shape
    blocks = act.reshape(chans, planes // 2, 2, rows // 2, 2, depth // 2, 2)
    return jnp.mean(blocks, axis=(2, 4, 6))


def by_halos(volume, weight_first, weight_deep, cotangent):
    planes, rows, depth = volume.shape[1:]
    rimmed = padded_2(volume, (("space", 1), ("chan", 2)), 1)
    padded = jnp.pad(rimmed, ((0, 0), (0, 0), (0, 0), (1, 1)))
    pre_first = convolve(padded, weight_first, planes, rows, depth)
    pooled = pool_mean(jax.nn.silu(pre_first)).astype(jnp.bfloat16)
    whole = lax.all_gather(pooled, "chan", axis=2, tiled=True)
    framed = padded_2(whole, (("space", 1),), 1)
    deep_in = jnp.pad(framed, ((0, 0), (0, 0), (1, 1), (1, 1)))
    deep_planes = pooled.shape[1]
    deep_rows, deep_depth = framed.shape[2:]
    pre_deep = convolve(deep_in, weight_deep, deep_planes, deep_rows, deep_depth)
    deep_out = jax.nn.silu(pre_deep).astype(jnp.bfloat16).reshape(cotangent.shape)
    sigma = jax.nn.sigmoid(pre_deep)
    cot_grid = cotangent.reshape(pre_deep.shape).astype(jnp.float32)
    grad_pre = (cot_grid * sigma * (1.0 + pre_deep * (1.0 - sigma))).astype(jnp.bfloat16)
    local_grad = weight_terms(grad_pre, deep_in, deep_planes, deep_rows, deep_depth)
    return deep_out, lax.psum(local_grad, "space")


DN = (((1,), (0,)), ((), ()))
NT = (((1,), (1,)), ((), ()))


def first_kernel(chans, place_ref, w_ref, *refs):
    pieces, (out_ref, grid, moved, patches) = refs[:chans], refs[chans:]
    planes, rows, cin, depth = grid.shape
    cmid = w_ref.shape[0]
    mine = place_ref[0]
    edge = jnp.zeros((cin, depth), jnp.bfloat16)
    for plane in range(planes):
        grid[plane, 0] = edge
        grid[plane, rows - 1] = edge
    for k in range(chans):
        per = pieces[k].shape[1]
        start = 1 + (mine ^ k) * per
        for plane in range(planes):
            for row in range(per):
                grid[plane, start + row] = pieces[k][plane, row]
    lane = lax.broadcasted_iota(jnp.int32, (rows * cin, depth), 1)
    for plane in range(planes):
        flat = grid[plane].reshape(rows * cin, depth).astype(jnp.float32)
        left = jnp.where(lane == 0, 0.0, pltpu.roll(flat, 1, 1))
        right = jnp.where(lane == depth - 1, 0.0, pltpu.roll(flat, depth - 1, 1))
        moved[0, plane] = left.astype(jnp.bfloat16).reshape(rows, cin, depth)
        moved[1, plane] = right.astype(jnp.bfloat16).reshape(rows, cin, depth)
    pair_rows = (rows - 2) // 2
    sums = []
    for pair in range(pair_rows):
        for a in range(3):
            for b in range(3):
                for c in range(3):
                    at = ((a * 3 + b) * 3 + c) * cin
                    for px in range(2):
                        for py in range(2):
                            x, y = px + a, 2 * pair + py + b
                            col = ((pair * 2 + px) * 2 + py) * depth
                            block = grid[x, y] if c == 1 else moved[c // 2, x, y]
                            patches[at : at + cin, col : col + depth] = block
        cols = patches[:, pair * 4 * depth : (pair + 1) * 4 * depth]
        pre = lax.dot_general(w_ref[...], cols, DN, preferred_element_type=jnp.float32)
        act = pre / (1.0 + jnp.exp(-pre))
        total = act[:, :depth]
        for part in range(1, 4):
            total = total + act[:, part * depth : (part + 1) * depth]
        sums.append(total * 0.125)
    fold_in = lax.broadcasted_iota(jnp.int32, (2 * depth, depth), 0)
    fold_out = lax.broadcasted_iota(jnp.int32, (2 * depth, depth), 1)
    fold = (fold_in // 2 == fold_out).astype(jnp.float32)
    for pair in range(0, pair_rows, 2):
        both = jnp.concatenate([sums[pair], sums[pair + 1]], axis=1)
        halved = lax.dot_general(
            both, fold, DN, precision=lax.Precision.HIGHEST, preferred_element_type=jnp.float32
        )
        out_ref[:, pair // 2 * depth : (pair // 2 + 1) * depth] = halved.astype(jnp.bfloat16)


def deep_kernel(groups, rowlen, place_ref, w_ref, *refs):
    same, refs = refs[:groups], refs[groups:]
    other, refs = refs[:groups], refs[groups:]
    cots, refs = refs[:groups], refs[groups:]
    out_ref, grad_ref, held, cot, pre, tap_same, tap_other = refs
    cmid, cells = same[0].shape
    mine = place_ref[0] // 2
    odd = place_ref[0] % 2
    held[groups] = jnp.zeros((cmid, cells), jnp.bfloat16)
    held[2 * groups] = jnp.zeros((cmid, cells), jnp.bfloat16)
    for k in range(groups):
        held[mine ^ k] = same[k][...]
        held[groups + (mine ^ k) + 1 - odd] = other[k][...]
        cot[mine ^ k] = cots[k][...]
    lane = lax.broadcasted_iota(jnp.int32, (cmid, cells), 1)
    z = lane % rowlen
    for slot in range(2 * groups + 1):
        plane = held[slot].astype(jnp.float32)
        target, at = (tap_same, slot) if slot < groups else (tap_other, slot - groups)
        for b in range(3):
            for c in range(3):
                shift = (b - 1) * rowlen + (c - 1)
                value = plane
                if shift:
                    value = pltpu.roll(plane, (-shift) % cells, 1)
                    ok = None
                    if b == 0:
                        ok = lane >= rowlen
                    if b == 2:
                        ok = lane < cells - rowlen
                    if c != 1:
                        inside = z > 0 if c == 0 else z < rowlen - 1
                        ok = inside if ok is None else ok & inside
                    value = jnp.where(ok, value, 0.0)
                row = (b * 3 + c) * cmid
                target[row : row + cmid, at * cells : (at + 1) * cells] = value.astype(jnp.bfloat16)
    width = groups * cells
    views = (
        tap_other.at[:, :width],
        tap_same.at[:, :],
        tap_other.at[:, cells : cells + width],
    )
    depth = tap_same.shape[0]
    total = None
    for a in range(3):
        term = lax.dot_general(
            w_ref[:, a * depth : (a + 1) * depth], views[a][...], DN, preferred_element_type=jnp.float32
        )
        total = term if total is None else total + term
    grads = []
    for k in range(groups):
        value = total[:, k * cells : (k + 1) * cells]
        sigma = 1.0 / (1.0 + jnp.exp(-value))
        pre[k] = (value * sigma).astype(jnp.bfloat16)
        grads.append(
            (cot[k].astype(jnp.float32) * sigma * (1.0 + value * (1.0 - sigma))).astype(jnp.bfloat16)
        )
    out_ref[...] = pre[mine]
    grad_pre = jnp.concatenate(grads, axis=1)
    for a in range(3):
        grad_ref[a * depth : (a + 1) * depth] = lax.dot_general(
            views[a][...], grad_pre, NT, preferred_element_type=jnp.float32
        )


def swap(array, axis, bits):
    peers = lax.axis_size(axis)
    return lax.ppermute(array, axis, [(i, i ^ bits) for i in range(peers)])


def by_gather(volume, weight_first, weight_deep, cotangent):
    cin, planes, rows, depth = volume.shape
    spaces, chans = lax.axis_size("space"), lax.axis_size("chan")
    groups = spaces // 2
    cmid = weight_first.shape[3]
    cout = weight_deep.shape[3]
    cells = cotangent.shape[2]
    at_space, at_chan = lax.axis_index("space"), lax.axis_index("chan")
    odd = at_space % 2 == 1

    block = jnp.transpose(volume, (1, 2, 0, 3))
    first, last = block[0], block[planes - 1]
    near = swap(jnp.where(odd, first, last), "space", 1)
    pairs = [(i, i + 1) for i in range(1, spaces - 1, 2)]
    far = lax.ppermute(jnp.where(odd, last, first), "space", pairs + [(j, i) for i, j in pairs])
    before, after = jnp.where(odd, near, far), jnp.where(odd, far, near)
    slab = jnp.concatenate([before[None], block, after[None]], axis=0)
    slabs = [slab] + [swap(slab, "chan", k) for k in range(1, chans)]

    cots = cotangent[:, 0]
    all_cots = [cots] + [swap(cots, "space", 2 * k) for k in range(1, groups)]

    taps_first = jnp.transpose(weight_first, (3, 0, 1, 2, 4)).reshape(cmid, 27 * cin)
    taps_deep = jnp.transpose(weight_deep, (3, 0, 1, 2, 4)).reshape(cout, 27 * cmid)

    all_rows = chans * rows
    vmem = pl.BlockSpec(memory_space=pltpu.VMEM)
    smem = pl.BlockSpec(memory_space=pltpu.SMEM)
    pooled = pl.pallas_call(
        functools.partial(first_kernel, chans),
        out_shape=jax.ShapeDtypeStruct((cmid, all_rows * depth // 4), jnp.bfloat16),
        in_specs=[smem, vmem] + [vmem] * chans,
        out_specs=vmem,
        scratch_shapes=[
            pltpu.VMEM((planes + 2, all_rows + 2, cin, depth), jnp.bfloat16),
            pltpu.VMEM((2, planes + 2, all_rows + 2, cin, depth), jnp.bfloat16),
            pltpu.VMEM((27 * cin, planes * all_rows * depth), jnp.bfloat16),
        ],
        compiler_params=pltpu.CompilerParams(vmem_limit_bytes=32 * 2**20),
        name="first",
    )(at_chan.reshape(1), taps_first, *slabs)

    same = [pooled] + [swap(pooled, "space", 2 * k) for k in range(1, groups)]
    other = [swap(p, "space", 1) for p in same]

    deep_out, terms = pl.pallas_call(
        functools.partial(deep_kernel, groups, depth // 2),
        out_shape=(
            jax.ShapeDtypeStruct((cout, cells), jnp.bfloat16),
            jax.ShapeDtypeStruct((27 * cmid, cout), jnp.float32),
        ),
        in_specs=[smem, vmem] + [vmem] * (3 * groups),
        out_specs=(vmem, vmem),
        scratch_shapes=[
            pltpu.VMEM((2 * groups + 1, cmid, cells), jnp.bfloat16),
            pltpu.VMEM((groups, cout, cells), jnp.bfloat16),
            pltpu.VMEM((groups, cout, cells), jnp.bfloat16),
            pltpu.VMEM((9 * cmid, groups * cells), jnp.bfloat16),
            pltpu.VMEM((9 * cmid, (groups + 1) * cells), jnp.bfloat16),
        ],
        compiler_params=pltpu.CompilerParams(vmem_limit_bytes=32 * 2**20),
        name="deep",
    )(at_space.reshape(1), taps_deep, *same, *other, *all_cots)

    grad = terms + swap(terms, "space", 1)
    grad = jnp.transpose(grad.reshape(3, 3, 3, cmid, cout), (0, 1, 2, 4, 3))
    return deep_out[:, None], grad


def on_device(volume, weight_first, weight_deep, cotangent):
    spaces, chans = lax.axis_size("space"), lax.axis_size("chan")
    powers = spaces & (spaces - 1) == 0 and chans & (chans - 1) == 0
    fits = spaces * cotangent.shape[0] * cotangent.shape[2] <= 2**20
    if powers and fits and spaces > 1 and volume.shape[1:3] == (2, 2):
        return by_gather(volume, weight_first, weight_deep, cotangent)
    return by_halos(volume, weight_first, weight_deep, cotangent)


def solution(mesh):
    return jax.shard_map(
        on_device,
        mesh=mesh,
        in_specs=(
            P(None, "space", "chan", None),
            P(),
            P(None, None, None, "chan", None),
            P("chan", "space", None),
        ),
        out_specs=(P("chan", "space", None), P(None, None, None, "chan", None)),
        check_vma=False,
    )
```

```python
import functools

import jax
import jax.numpy as jnp
from jax import lax
from jax.experimental import pallas as pl
from jax.experimental.pallas import tpu as pltpu
from jax.sharding import PartitionSpec as P


def padded_2(array, sides, width):
    for axis, dim in sides:
        peers, length = (lax.axis_size(axis), array.shape[dim])
        up = [(i, (i + 1) % peers) for i in range(peers - 1)]
        down = [(j, i) for i, j in up]
        last = lax.slice_in_dim(array, length - width, length, axis=dim)
        leading = lax.slice_in_dim(array, 0, width, axis=dim)
        before = lax.ppermute(last, axis, up)
        after = lax.ppermute(leading, axis, down)
        array = jnp.concatenate([before, array, after], axis=dim)
    return array


def windows(padded, planes, rows, depth):
    for offset_x in range(3):
        for offset_y in range(3):
            for offset_z in range(3):
                yield (offset_x, offset_y, offset_z), padded[
                    :,
                    offset_x : offset_x + planes,
                    offset_y : offset_y + rows,
                    offset_z : offset_z + depth,
                ]


def convolve(padded, weight, planes, rows, depth):
    total = jnp.zeros((weight.shape[3], planes, rows, depth), jnp.float32)
    for tap, window in windows(padded, planes, rows, depth):
        total = total + jnp.einsum(
            "oc,cxyz->oxyz", weight[tap], window, preferred_element_type=jnp.float32
        )
    return total


def weight_terms(grad_pre, padded, planes, rows, depth):
    terms = [
        jnp.einsum("oxyz,cxyz->oc", grad_pre, window, preferred_element_type=jnp.float32)
        for _, window in windows(padded, planes, rows, depth)
    ]
    return jnp.stack(terms).reshape((3, 3, 3) + terms[0].shape)


def pool_mean(act):
    chans, planes, rows, depth = act.shape
    blocks = act.reshape(chans, planes // 2, 2, rows // 2, 2, depth // 2, 2)
    return jnp.mean(blocks, axis=(2, 4, 6))


def by_halos(volume, weight_first, weight_deep, cotangent):
    planes, rows, depth = volume.shape[1:]
    rimmed = padded_2(volume, (("space", 1), ("chan", 2)), 1)
    padded = jnp.pad(rimmed, ((0, 0), (0, 0), (0, 0), (1, 1)))
    pre_first = convolve(padded, weight_first, planes, rows, depth)
    pooled = pool_mean(jax.nn.silu(pre_first)).astype(jnp.bfloat16)
    whole = lax.all_gather(pooled, "chan", axis=2, tiled=True)
    framed = padded_2(whole, (("space", 1),), 1)
    deep_in = jnp.pad(framed, ((0, 0), (0, 0), (1, 1), (1, 1)))
    deep_planes = pooled.shape[1]
    deep_rows, deep_depth = framed.shape[2:]
    pre_deep = convolve(deep_in, weight_deep, deep_planes, deep_rows, deep_depth)
    deep_out = jax.nn.silu(pre_deep).astype(jnp.bfloat16).reshape(cotangent.shape)
    sigma = jax.nn.sigmoid(pre_deep)
    cot_grid = cotangent.reshape(pre_deep.shape).astype(jnp.float32)
    grad_pre = (cot_grid * sigma * (1.0 + pre_deep * (1.0 - sigma))).astype(jnp.bfloat16)
    local_grad = weight_terms(grad_pre, deep_in, deep_planes, deep_rows, deep_depth)
    return deep_out, lax.psum(local_grad, "space")


DN = (((1,), (0,)), ((), ()))
NT = (((1,), (1,)), ((), ()))
TN = (((0,), (0,)), ((), ()))


def fill_patches(grid, moved, patches):
    planes, rows, cin, depth = grid.shape
    lane = lax.broadcasted_iota(jnp.int32, (rows * cin, depth), 1)
    for plane in range(planes):
        flat = grid[plane].reshape(rows * cin, depth).astype(jnp.float32)
        left = jnp.where(lane == 0, 0.0, pltpu.roll(flat, 1, 1))
        right = jnp.where(lane == depth - 1, 0.0, pltpu.roll(flat, depth - 1, 1))
        moved[0, plane] = left.astype(jnp.bfloat16).reshape(rows, cin, depth)
        moved[1, plane] = right.astype(jnp.bfloat16).reshape(rows, cin, depth)
    for plane in range(planes):
        for b in range(3):
            for c in range(3):
                at = ((plane * 3 + b) * 3 + c) * cin
                for row in range(rows - 2):
                    block = grid[plane, row + b] if c == 1 else moved[c // 2, plane, row + b]
                    patches[at : at + cin, row * depth : (row + 1) * depth] = block


def silu(value):
    return value / (1.0 + jnp.exp(-value))


def first_part(chans, place_ref, w_ref, near_ref, *refs):
    blocks, (part_ref, sums_ref, grid, moved, patches) = refs[:chans], refs[-5:]
    planes, rows, cin, depth = grid.shape
    mine, odd = place_ref[0], place_ref[1]
    edge = jnp.zeros((cin, depth), jnp.bfloat16)
    for plane in range(planes):
        grid[plane, 0] = edge
        grid[plane, rows - 1] = edge
    for k in range(chans):
        per = near_ref.shape[1]
        start = 1 + (mine ^ k) * per
        for row in range(per):
            grid[0, start + row] = blocks[k][odd, row]
            grid[1, start + row] = blocks[k][1 - odd, row]
            grid[2, start + row] = near_ref[k, row]
    fill_patches(grid, moved, patches)
    to_far, centre, from_far = w_ref[2 * odd], w_ref[1], w_ref[2 - 2 * odd]
    inner = jnp.concatenate([to_far, centre, from_far], axis=0)
    outer = jnp.concatenate([centre, from_far], axis=0)
    for pair in range((rows - 2) // 2):
        cols = slice(pair * 2 * depth, (pair + 1) * 2 * depth)
        act = silu(lax.dot_general(inner, patches[:, cols], TN, preferred_element_type=jnp.float32))
        sums_ref[:, pair * depth : (pair + 1) * depth] = act[:, :depth] + act[:, depth:]
        part_ref[:, cols] = lax.dot_general(
            outer, patches[: outer.shape[0], cols], TN, preferred_element_type=jnp.float32
        )


def first_rest(place_ref, w_ref, far_ref, part_ref, sums_ref, *refs):
    out_ref, grid, moved, patches = refs[-4:]
    _, rows, cin, depth = grid.shape
    mine, odd, has_far = place_ref[0], place_ref[1], place_ref[2] == 1
    edge = jnp.zeros((cin, depth), jnp.bfloat16)
    grid[0, 0] = edge
    grid[0, rows - 1] = edge
    per = far_ref.shape[1]
    for k in range(far_ref.shape[0]):
        for row in range(per):
            grid[0, 1 + (mine ^ k) * per + row] = jnp.where(has_far, far_ref[k, row], edge)
    fill_patches(grid, moved, patches)
    to_far = w_ref[2 * odd]
    sums = []
    for pair in range((rows - 2) // 2):
        cols = slice(pair * 2 * depth, (pair + 1) * 2 * depth)
        term = lax.dot_general(to_far, patches[:, cols], TN, preferred_element_type=jnp.float32)
        act = silu(part_ref[:, cols] + term)
        total = sums_ref[:, pair * depth : (pair + 1) * depth] + act[:, :depth] + act[:, depth:]
        sums.append(total * 0.125)
    fold_in = lax.broadcasted_iota(jnp.int32, (2 * depth, depth), 0)
    fold_out = lax.broadcasted_iota(jnp.int32, (2 * depth, depth), 1)
    fold = (fold_in // 2 == fold_out).astype(jnp.float32)
    for pair in range(0, len(sums), 2):
        both = jnp.concatenate([sums[pair], sums[pair + 1]], axis=1)
        halved = lax.dot_general(
            both, fold, DN, precision=lax.Precision.HIGHEST, preferred_element_type=jnp.float32
        )
        out_ref[:, pair // 2 * depth : (pair // 2 + 1) * depth] = halved.astype(jnp.bfloat16)


def deep_kernel(rowlen, order, place_ref, w_ref, cot_ref, cot_swapped_ref, *refs):
    count = len(refs) - 7
    planes, refs = refs[:count], refs[count:]
    out_ref, grad_ref, held, cot, act, taps, shifted = refs
    cmid, cells = held.shape[1:]
    cout = cot.shape[1]
    mine = place_ref[0]
    for k in range(count):
        held[mine ^ 1 ^ k] = planes[k][...]
    for k, bits in enumerate(order):
        cot[mine ^ bits] = cot_ref[k]
        cot[mine ^ bits ^ 1] = cot_swapped_ref[k]
    lane = lax.broadcasted_iota(jnp.int32, (cmid, cells), 1)
    z = lane % rowlen
    edge = jnp.zeros((9 * cmid, cells), jnp.bfloat16)
    taps[:, :cells] = edge
    taps[:, (count + 1) * cells :] = edge
    for slot in range(count):
        plane = held[slot].astype(jnp.float32)
        for b in range(3):
            for c in range(3):
                shift = (b - 1) * rowlen + (c - 1)
                value = plane
                if shift:
                    value = pltpu.roll(plane, (-shift) % cells, 1)
                    ok = None
                    if b == 0:
                        ok = lane >= rowlen
                    if b == 2:
                        ok = lane < cells - rowlen
                    if c != 1:
                        inside = z > 0 if c == 0 else z < rowlen - 1
                        ok = inside if ok is None else ok & inside
                    value = jnp.where(ok, value, 0.0)
                row = (b * 3 + c) * cmid
                taps[row : row + cmid, (slot + 1) * cells : (slot + 2) * cells] = value.astype(jnp.bfloat16)
    depth = 9 * cmid
    empty = jnp.zeros((cout, cells), jnp.bfloat16)
    for p in range(count):
        rhs = jnp.concatenate(
            [taps[:, (p + a) * cells : (p + a + 1) * cells] for a in range(3)], axis=0
        )
        value = lax.dot_general(w_ref[...], rhs, DN, preferred_element_type=jnp.float32)
        sigma = 1.0 / (1.0 + jnp.exp(-value))
        act[p] = (value * sigma).astype(jnp.bfloat16)
        grad_pre = cot[p].astype(jnp.float32) * sigma * (1.0 + value * (1.0 - sigma))
        for a in range(3):
            q = p + a - 1
            if 0 <= q < count:
                shifted[a * cout : (a + 1) * cout, q * cells : (q + 1) * cells] = grad_pre.astype(
                    jnp.bfloat16
                )
    shifted[:cout, (count - 1) * cells :] = empty
    shifted[2 * cout :, :cells] = empty
    out_ref[...] = act[mine]
    half = depth // 2
    for row in range(0, depth, half):
        terms = lax.dot_general(
            taps[row : row + half, cells : (count + 1) * cells],
            shifted[...],
            NT,
            preferred_element_type=jnp.float32,
        )
        for a in range(3):
            at = a * depth + row
            grad_ref[at : at + half] = terms[:, a * cout : (a + 1) * cout]


def swap(array, axis, bits):
    peers = lax.axis_size(axis)
    return lax.ppermute(array, axis, [(i, i ^ bits) for i in range(peers)])


def crossed(array, bits):
    spaces, chans = lax.axis_size("space"), lax.axis_size("chan")
    pairs = [(s * chans + c, (s ^ 1) * chans + (c ^ bits)) for s in range(spaces) for c in range(chans)]
    return lax.ppermute(array, ("space", "chan"), pairs)


def spread(array, order):
    direct = [swap(array, "space", bits) if bits else array for bits in order]
    pieces = {}
    for bits, piece in zip(order, direct):
        pieces[bits], pieces[bits ^ 1] = piece, swap(piece, "space", 1)
    return [pieces[k] for k in range(2 * len(order))]


def by_gather(volume, weight_first, weight_deep, cotangent):
    cin, planes, rows, depth = volume.shape
    spaces, chans = lax.axis_size("space"), lax.axis_size("chan")
    cmid, cout, cells = weight_first.shape[3], weight_deep.shape[3], cotangent.shape[2]
    all_rows = chans * rows
    at_space, at_chan = lax.axis_index("space"), lax.axis_index("chan")
    role = at_space ^ 1
    odd = role % 2
    order = [k | k.bit_count() % 2 for k in range(0, spaces, 2)]
    vmem, smem = pl.BlockSpec(memory_space=pltpu.VMEM), pl.BlockSpec(memory_space=pltpu.SMEM)
    unread = pl.BlockSpec(memory_space=pl.ANY)

    block = jnp.transpose(volume, (1, 2, 0, 3))
    blocks = [crossed(block, k) for k in range(chans)]
    first = jnp.stack([piece[0] for piece in blocks])
    last = jnp.stack([piece[planes - 1] for piece in blocks])
    near = swap(jnp.where(odd == 1, first, last), "space", 1)
    pairs = [(i ^ 1, ((i + 1) % spaces) ^ 1) for i in range(1, spaces, 2)]
    far = lax.ppermute(
        jnp.where(odd == 1, last, first), "space", pairs + [(j, i) for i, j in pairs]
    )
    has_far = ((role > 0) & (role < spaces - 1)).astype(jnp.int32)
    place = jnp.stack([at_chan, odd, has_far])

    cots = [cotangent[:, 0]]
    cots = cots + [swap(cots[0], "space", bits) for bits in order[1:]]

    taps_first = jnp.transpose(weight_first, (0, 1, 2, 4, 3)).reshape(3, 9 * cin, cmid)

    def patch_scratch(count):
        return [
            pltpu.VMEM((count, all_rows + 2, cin, depth), jnp.bfloat16),
            pltpu.VMEM((2, count, all_rows + 2, cin, depth), jnp.bfloat16),
            pltpu.VMEM((count * 9 * cin, all_rows * depth), jnp.bfloat16),
        ]

    params = pltpu.CompilerParams(vmem_limit_bytes=32 * 2**20)
    part, sums = pl.pallas_call(
        functools.partial(first_part, chans),
        out_shape=(
            jax.ShapeDtypeStruct((cmid, all_rows * depth), jnp.float32),
            jax.ShapeDtypeStruct((cmid, all_rows * depth // 2), jnp.float32),
        ),
        in_specs=[smem, vmem, vmem] + [vmem] * chans,
        out_specs=(vmem, vmem),
        scratch_shapes=patch_scratch(planes + 1),
        compiler_params=params,
        name="first_part",
        cost_estimate=pl.CostEstimate(flops=0, bytes_accessed=5000000, transcendentals=0),
    )(place, taps_first, near, *blocks)

    pooled = pl.pallas_call(
        first_rest,
        out_shape=jax.ShapeDtypeStruct((cmid, cells), jnp.bfloat16),
        in_specs=[smem, vmem, vmem, vmem, vmem],
        out_specs=vmem,
        scratch_shapes=patch_scratch(1),
        compiler_params=params,
        name="first_rest",
        cost_estimate=pl.CostEstimate(flops=0, bytes_accessed=4000000, transcendentals=0),
    )(place, taps_first, far, part, sums)

    pooled, weight_deep, *cots = lax.optimization_barrier((pooled, weight_deep, *cots))
    taps_deep = jnp.transpose(weight_deep, (3, 0, 1, 2, 4)).reshape(cout, 27 * cmid)
    cots = jnp.stack(cots)
    cots_swapped = swap(cots, "space", 1)
    all_pooled = spread(pooled, order)

    deep_out, terms = pl.pallas_call(
        functools.partial(deep_kernel, depth // 2, order),
        out_shape=(
            jax.ShapeDtypeStruct((cout, cells), jnp.bfloat16),
            jax.ShapeDtypeStruct((27 * cmid, cout), jnp.float32),
        ),
        in_specs=[smem] + [vmem] * (3 + spaces),
        out_specs=(vmem, vmem),
        scratch_shapes=[
            pltpu.VMEM((spaces, cmid, cells), jnp.bfloat16),
            pltpu.VMEM((spaces, cout, cells), jnp.bfloat16),
            pltpu.VMEM((spaces, cout, cells), jnp.bfloat16),
            pltpu.VMEM((9 * cmid, (spaces + 2) * cells), jnp.bfloat16),
            pltpu.VMEM((3 * cout, spaces * cells), jnp.bfloat16),
        ],
        compiler_params=params,
        name="deep",
        cost_estimate=pl.CostEstimate(flops=0, bytes_accessed=12000000, transcendentals=0),
    )(at_space.reshape(1), taps_deep, cots, cots_swapped, *all_pooled)

    grad = jnp.transpose(terms.reshape(3, 3, 3, cmid, cout), (0, 1, 2, 4, 3))
    return deep_out[:, None], grad


def on_device(volume, weight_first, weight_deep, cotangent):
    spaces, chans = lax.axis_size("space"), lax.axis_size("chan")
    powers = spaces & (spaces - 1) == 0 and chans & (chans - 1) == 0
    fits = spaces * cotangent.shape[0] * cotangent.shape[2] <= 2**20
    if powers and fits and spaces > 1 and volume.shape[1:3] == (2, 2):
        return by_gather(volume, weight_first, weight_deep, cotangent)
    return by_halos(volume, weight_first, weight_deep, cotangent)


def solution(mesh):
    return jax.shard_map(
        on_device,
        mesh=mesh,
        in_specs=(
            P(None, "space", "chan", None),
            P(),
            P(None, None, None, "chan", None),
            P("chan", "space", None),
        ),
        out_specs=(P("chan", "space", None), P(None, None, None, "chan", None)),
        check_vma=False,
    )
```

```python
import functools

import jax
import jax.numpy as jnp
from jax import lax
from jax.experimental import pallas as pl
from jax.experimental.pallas import tpu as pltpu
from jax.sharding import PartitionSpec as P


def padded_2(array, sides, width):
    for axis, dim in sides:
        peers, length = (lax.axis_size(axis), array.shape[dim])
        up = [(i, (i + 1) % peers) for i in range(peers - 1)]
        down = [(j, i) for i, j in up]
        last = lax.slice_in_dim(array, length - width, length, axis=dim)
        leading = lax.slice_in_dim(array, 0, width, axis=dim)
        before = lax.ppermute(last, axis, up)
        after = lax.ppermute(leading, axis, down)
        array = jnp.concatenate([before, array, after], axis=dim)
    return array


def windows(padded, planes, rows, depth):
    for offset_x in range(3):
        for offset_y in range(3):
            for offset_z in range(3):
                yield (offset_x, offset_y, offset_z), padded[
                    :,
                    offset_x : offset_x + planes,
                    offset_y : offset_y + rows,
                    offset_z : offset_z + depth,
                ]


def convolve(padded, weight, planes, rows, depth):
    total = jnp.zeros((weight.shape[3], planes, rows, depth), jnp.float32)
    for tap, window in windows(padded, planes, rows, depth):
        total = total + jnp.einsum(
            "oc,cxyz->oxyz", weight[tap], window, preferred_element_type=jnp.float32
        )
    return total


def weight_terms(grad_pre, padded, planes, rows, depth):
    terms = [
        jnp.einsum("oxyz,cxyz->oc", grad_pre, window, preferred_element_type=jnp.float32)
        for _, window in windows(padded, planes, rows, depth)
    ]
    return jnp.stack(terms).reshape((3, 3, 3) + terms[0].shape)


def pool_mean(act):
    chans, planes, rows, depth = act.shape
    blocks = act.reshape(chans, planes // 2, 2, rows // 2, 2, depth // 2, 2)
    return jnp.mean(blocks, axis=(2, 4, 6))


def by_halos(volume, weight_first, weight_deep, cotangent):
    planes, rows, depth = volume.shape[1:]
    rimmed = padded_2(volume, (("space", 1), ("chan", 2)), 1)
    padded = jnp.pad(rimmed, ((0, 0), (0, 0), (0, 0), (1, 1)))
    pre_first = convolve(padded, weight_first, planes, rows, depth)
    pooled = pool_mean(jax.nn.silu(pre_first)).astype(jnp.bfloat16)
    whole = lax.all_gather(pooled, "chan", axis=2, tiled=True)
    framed = padded_2(whole, (("space", 1),), 1)
    deep_in = jnp.pad(framed, ((0, 0), (0, 0), (1, 1), (1, 1)))
    deep_planes = pooled.shape[1]
    deep_rows, deep_depth = framed.shape[2:]
    pre_deep = convolve(deep_in, weight_deep, deep_planes, deep_rows, deep_depth)
    deep_out = jax.nn.silu(pre_deep).astype(jnp.bfloat16).reshape(cotangent.shape)
    sigma = jax.nn.sigmoid(pre_deep)
    cot_grid = cotangent.reshape(pre_deep.shape).astype(jnp.float32)
    grad_pre = (cot_grid * sigma * (1.0 + pre_deep * (1.0 - sigma))).astype(jnp.bfloat16)
    local_grad = weight_terms(grad_pre, deep_in, deep_planes, deep_rows, deep_depth)
    return deep_out, lax.psum(local_grad, "space")


DN = (((1,), (0,)), ((), ()))
NT = (((1,), (1,)), ((), ()))
TN = (((0,), (0,)), ((), ()))


def place():
    role = lax.axis_index("space") ^ 1
    return lax.axis_index("chan"), role & 1, (role > 0) & (role < lax.axis_size("space") - 1)


def fill_patches(grid, moved, patches):
    planes, rows, cin, depth = grid.shape
    lane = lax.broadcasted_iota(jnp.int32, (rows * cin, depth), 1)
    for plane in range(planes):
        flat = grid[plane].reshape(rows * cin, depth).astype(jnp.float32)
        left = jnp.where(lane == 0, 0.0, pltpu.roll(flat, 1, 1))
        right = jnp.where(lane == depth - 1, 0.0, pltpu.roll(flat, depth - 1, 1))
        moved[0, plane] = left.astype(jnp.bfloat16).reshape(rows, cin, depth)
        moved[1, plane] = right.astype(jnp.bfloat16).reshape(rows, cin, depth)
    for plane in range(planes):
        for b in range(3):
            for c in range(3):
                at = ((plane * 3 + b) * 3 + c) * cin
                for row in range(rows - 2):
                    block = grid[plane, row + b] if c == 1 else moved[c // 2, plane, row + b]
                    patches[at : at + cin, row * depth : (row + 1) * depth] = block


def silu(value):
    return value / (1.0 + jnp.exp(-value))


def first_part(chans, w_ref, near_ref, *refs):
    blocks, (part_ref, sums_ref, grid, moved, patches) = refs[:chans], refs[-5:]
    planes, rows, cin, depth = grid.shape
    mine, odd, _ = place()
    edge = jnp.zeros((cin, depth), jnp.bfloat16)
    for plane in range(planes):
        grid[plane, 0] = edge
        grid[plane, rows - 1] = edge
    for k in range(chans):
        per = near_ref.shape[1]
        start = 1 + (mine ^ k) * per
        for row in range(per):
            grid[0, start + row] = blocks[k][odd, row]
            grid[1, start + row] = blocks[k][1 - odd, row]
            grid[2, start + row] = near_ref[k, row]
    fill_patches(grid, moved, patches)
    to_far, centre, from_far = w_ref[2 * odd], w_ref[1], w_ref[2 - 2 * odd]
    inner = jnp.concatenate([to_far, centre, from_far], axis=0)
    outer = jnp.concatenate([centre, from_far], axis=0)
    for pair in range((rows - 2) // 2):
        cols = slice(pair * 2 * depth, (pair + 1) * 2 * depth)
        act = silu(lax.dot_general(inner, patches[:, cols], TN, preferred_element_type=jnp.float32))
        sums_ref[:, pair * depth : (pair + 1) * depth] = act[:, :depth] + act[:, depth:]
        part_ref[:, cols] = lax.dot_general(
            outer, patches[: outer.shape[0], cols], TN, preferred_element_type=jnp.float32
        )


def first_rest(w_ref, far_ref, part_ref, sums_ref, *refs):
    out_ref, grid, moved, patches = refs[-4:]
    _, rows, cin, depth = grid.shape
    mine, odd, has_far = place()
    edge = jnp.zeros((cin, depth), jnp.bfloat16)
    grid[0, 0] = edge
    grid[0, rows - 1] = edge
    per = far_ref.shape[1]
    for k in range(far_ref.shape[0]):
        for row in range(per):
            grid[0, 1 + (mine ^ k) * per + row] = jnp.where(has_far, far_ref[k, row], edge)
    fill_patches(grid, moved, patches)
    to_far = w_ref[2 * odd]
    sums = []
    for pair in range((rows - 2) // 2):
        cols = slice(pair * 2 * depth, (pair + 1) * 2 * depth)
        term = lax.dot_general(to_far, patches[:, cols], TN, preferred_element_type=jnp.float32)
        act = silu(part_ref[:, cols] + term)
        total = sums_ref[:, pair * depth : (pair + 1) * depth] + act[:, :depth] + act[:, depth:]
        sums.append(total * 0.125)
    fold_in = lax.broadcasted_iota(jnp.int32, (2 * depth, depth), 0)
    fold_out = lax.broadcasted_iota(jnp.int32, (2 * depth, depth), 1)
    fold = (fold_in // 2 == fold_out).astype(jnp.float32)
    for pair in range(0, len(sums), 2):
        both = jnp.concatenate([sums[pair], sums[pair + 1]], axis=1)
        halved = lax.dot_general(
            both, fold, DN, precision=lax.Precision.HIGHEST, preferred_element_type=jnp.float32
        )
        out_ref[:, pair // 2 * depth : (pair // 2 + 1) * depth] = halved.astype(jnp.bfloat16)


def deep_kernel(rowlen, order, w_ref, cot_ref, cot_swapped_ref, *refs):
    count = len(refs) - 7
    planes, refs = refs[:count], refs[count:]
    out_ref, grad_ref, held, cot, act, taps, shifted = refs
    cmid, cells = held.shape[1:]
    cout = cot.shape[1]
    mine = lax.axis_index("space")
    for k in range(count):
        held[mine ^ 1 ^ k] = planes[k][...]
    for k, bits in enumerate(order):
        cot[mine ^ bits] = cot_ref[k]
        cot[mine ^ bits ^ 1] = cot_swapped_ref[k]
    lane = lax.broadcasted_iota(jnp.int32, (cmid, cells), 1)
    z = lane % rowlen
    edge = jnp.zeros((9 * cmid, cells), jnp.bfloat16)
    taps[:, :cells] = edge
    taps[:, (count + 1) * cells :] = edge
    for slot in range(count):
        plane = held[slot].astype(jnp.float32)
        for b in range(3):
            for c in range(3):
                shift = (b - 1) * rowlen + (c - 1)
                value = plane
                if shift:
                    value = pltpu.roll(plane, (-shift) % cells, 1)
                    ok = None
                    if b == 0:
                        ok = lane >= rowlen
                    if b == 2:
                        ok = lane < cells - rowlen
                    if c != 1:
                        inside = z > 0 if c == 0 else z < rowlen - 1
                        ok = inside if ok is None else ok & inside
                    value = jnp.where(ok, value, 0.0)
                row = (b * 3 + c) * cmid
                taps[row : row + cmid, (slot + 1) * cells : (slot + 2) * cells] = value.astype(jnp.bfloat16)
    depth = 9 * cmid
    empty = jnp.zeros((cout, cells), jnp.bfloat16)
    for p in range(count):
        rhs = jnp.concatenate(
            [taps[:, (p + a) * cells : (p + a + 1) * cells] for a in range(3)], axis=0
        )
        value = lax.dot_general(w_ref[...], rhs, DN, preferred_element_type=jnp.float32)
        sigma = 1.0 / (1.0 + jnp.exp(-value))
        act[p] = (value * sigma).astype(jnp.bfloat16)
        grad_pre = cot[p].astype(jnp.float32) * sigma * (1.0 + value * (1.0 - sigma))
        for a in range(3):
            q = p + a - 1
            if 0 <= q < count:
                shifted[a * cout : (a + 1) * cout, q * cells : (q + 1) * cells] = grad_pre.astype(
                    jnp.bfloat16
                )
    shifted[:cout, (count - 1) * cells :] = empty
    shifted[2 * cout :, :cells] = empty
    out_ref[...] = act[mine]
    half = depth // 2
    for row in range(0, depth, half):
        terms = lax.dot_general(
            taps[row : row + half, cells : (count + 1) * cells],
            shifted[...],
            NT,
            preferred_element_type=jnp.float32,
        )
        for a in range(3):
            at = a * depth + row
            grad_ref[at : at + half] = terms[:, a * cout : (a + 1) * cout]


def after(event, *arrays):
    return lax.optimization_barrier((event, *arrays))[1:]


def swap(array, axis, bits):
    peers = lax.axis_size(axis)
    return lax.ppermute(array, axis, [(i, i ^ bits) for i in range(peers)])


def crossed(array, bits):
    spaces, chans = lax.axis_size("space"), lax.axis_size("chan")
    pairs = [(s * chans + c, (s ^ 1) * chans + (c ^ bits)) for s in range(spaces) for c in range(chans)]
    return lax.ppermute(array, ("space", "chan"), pairs)


def spread(direct, order):
    pieces = {}
    for bits, piece in zip(order, direct):
        pieces[bits], pieces[bits ^ 1] = piece, swap(piece, "space", 1)
    return [pieces[k] for k in range(2 * len(order))]


def by_gather(volume, weight_first, weight_deep, cotangent):
    cin, planes, rows, depth = volume.shape
    spaces, chans = lax.axis_size("space"), lax.axis_size("chan")
    cmid, cout, cells = weight_first.shape[3], weight_deep.shape[3], cotangent.shape[2]
    all_rows = chans * rows
    odd = (lax.axis_index("space") ^ 1) & 1
    order = [k | k.bit_count() % 2 for k in range(0, spaces, 2)]
    vmem = pl.BlockSpec(memory_space=pltpu.VMEM)

    block = jnp.transpose(volume, (1, 2, 0, 3))
    blocks = [crossed(block, k) for k in range(chans)]
    first = jnp.stack([piece[0] for piece in blocks])
    last = jnp.stack([piece[planes - 1] for piece in blocks])
    near = swap(jnp.where(odd == 1, first, last), "space", 1)
    pairs = [(i ^ 1, ((i + 1) % spaces) ^ 1) for i in range(1, spaces, 2)]
    far = lax.ppermute(
        jnp.where(odd == 1, last, first), "space", pairs + [(j, i) for i, j in pairs]
    )

    cots = [cotangent[:, 0]]
    cots = cots + [swap(cots[0], "space", bits) for bits in order[1:]]

    taps_first = jnp.transpose(weight_first, (0, 1, 2, 4, 3)).reshape(3, 9 * cin, cmid)

    def patch_scratch(count):
        return [
            pltpu.VMEM((count, all_rows + 2, cin, depth), jnp.bfloat16),
            pltpu.VMEM((2, count, all_rows + 2, cin, depth), jnp.bfloat16),
            pltpu.VMEM((count * 9 * cin, all_rows * depth), jnp.bfloat16),
        ]

    params = pltpu.CompilerParams(vmem_limit_bytes=32 * 2**20)
    part, sums = pl.pallas_call(
        functools.partial(first_part, chans),
        out_shape=(
            jax.ShapeDtypeStruct((cmid, all_rows * depth), jnp.float32),
            jax.ShapeDtypeStruct((cmid, all_rows * depth // 2), jnp.float32),
        ),
        in_specs=[vmem] * (2 + chans) + [pl.BlockSpec(memory_space=pl.ANY)] * (len(order) - 1),
        out_specs=(vmem, vmem),
        scratch_shapes=patch_scratch(planes + 1),
        compiler_params=params,
        name="first_part",
        cost_estimate=pl.CostEstimate(flops=0, bytes_accessed=5000000, transcendentals=0),
    )(taps_first, near, *blocks, *cots[1:])

    pooled = pl.pallas_call(
        first_rest,
        out_shape=jax.ShapeDtypeStruct((cmid, cells), jnp.bfloat16),
        in_specs=[vmem] * 4,
        out_specs=vmem,
        scratch_shapes=patch_scratch(1),
        compiler_params=params,
        name="first_rest",
        cost_estimate=pl.CostEstimate(flops=0, bytes_accessed=4000000, transcendentals=0),
    )(taps_first, far, part, sums)

    direct = [pooled] + [swap(pooled, "space", bits) for bits in order[1:]]
    (weight_deep,) = after(pooled, weight_deep)
    taps_deep = jnp.transpose(weight_deep, (3, 0, 1, 2, 4)).reshape(cout, 27 * cmid)
    cots = after(pooled, *cots)
    cots = jnp.stack(cots)
    cots_swapped = swap(cots, "space", 1)
    all_pooled = spread(direct, order)

    deep_out, terms = pl.pallas_call(
        functools.partial(deep_kernel, depth // 2, order),
        out_shape=(
            jax.ShapeDtypeStruct((cout, cells), jnp.bfloat16),
            jax.ShapeDtypeStruct((27 * cmid, cout), jnp.float32),
        ),
        in_specs=[vmem] * (3 + spaces),
        out_specs=(vmem, vmem),
        scratch_shapes=[
            pltpu.VMEM((spaces, cmid, cells), jnp.bfloat16),
            pltpu.VMEM((spaces, cout, cells), jnp.bfloat16),
            pltpu.VMEM((spaces, cout, cells), jnp.bfloat16),
            pltpu.VMEM((9 * cmid, (spaces + 2) * cells), jnp.bfloat16),
            pltpu.VMEM((3 * cout, spaces * cells), jnp.bfloat16),
        ],
        compiler_params=params,
        name="deep",
        cost_estimate=pl.CostEstimate(flops=0, bytes_accessed=12000000, transcendentals=0),
    )(taps_deep, cots, cots_swapped, *all_pooled)

    grad = jnp.transpose(terms.reshape(3, 3, 3, cmid, cout), (0, 1, 2, 4, 3))
    return deep_out[:, None], grad


def on_device(volume, weight_first, weight_deep, cotangent):
    spaces, chans = lax.axis_size("space"), lax.axis_size("chan")
    powers = spaces & (spaces - 1) == 0 and chans & (chans - 1) == 0
    fits = spaces * cotangent.shape[0] * cotangent.shape[2] <= 2**20
    if powers and fits and spaces > 1 and volume.shape[1:3] == (2, 2):
        return by_gather(volume, weight_first, weight_deep, cotangent)
    return by_halos(volume, weight_first, weight_deep, cotangent)


def solution(mesh):
    return jax.shard_map(
        on_device,
        mesh=mesh,
        in_specs=(
            P(None, "space", "chan", None),
            P(),
            P(None, None, None, "chan", None),
            P("chan", "space", None),
        ),
        out_specs=(P("chan", "space", None), P(None, None, None, "chan", None)),
        check_vma=False,
    )
```

```python
import functools

import jax
import jax.numpy as jnp
from jax import lax
from jax.experimental import pallas as pl
from jax.experimental.layout import Layout, with_layout_constraint
from jax.experimental.pallas import tpu as pltpu
from jax.sharding import PartitionSpec as P


def padded_2(array, sides, width):
    for axis, dim in sides:
        peers, length = (lax.axis_size(axis), array.shape[dim])
        up = [(i, (i + 1) % peers) for i in range(peers - 1)]
        down = [(j, i) for i, j in up]
        last = lax.slice_in_dim(array, length - width, length, axis=dim)
        leading = lax.slice_in_dim(array, 0, width, axis=dim)
        before = lax.ppermute(last, axis, up)
        after = lax.ppermute(leading, axis, down)
        array = jnp.concatenate([before, array, after], axis=dim)
    return array


def windows(padded, planes, rows, depth):
    for offset_x in range(3):
        for offset_y in range(3):
            for offset_z in range(3):
                yield (offset_x, offset_y, offset_z), padded[
                    :,
                    offset_x : offset_x + planes,
                    offset_y : offset_y + rows,
                    offset_z : offset_z + depth,
                ]


def convolve(padded, weight, planes, rows, depth):
    total = jnp.zeros((weight.shape[3], planes, rows, depth), jnp.float32)
    for tap, window in windows(padded, planes, rows, depth):
        total = total + jnp.einsum(
            "oc,cxyz->oxyz", weight[tap], window, preferred_element_type=jnp.float32
        )
    return total


def weight_terms(grad_pre, padded, planes, rows, depth):
    terms = [
        jnp.einsum("oxyz,cxyz->oc", grad_pre, window, preferred_element_type=jnp.float32)
        for _, window in windows(padded, planes, rows, depth)
    ]
    return jnp.stack(terms).reshape((3, 3, 3) + terms[0].shape)


def pool_mean(act):
    chans, planes, rows, depth = act.shape
    blocks = act.reshape(chans, planes // 2, 2, rows // 2, 2, depth // 2, 2)
    return jnp.mean(blocks, axis=(2, 4, 6))


def by_halos(volume, weight_first, weight_deep, cotangent):
    planes, rows, depth = volume.shape[1:]
    rimmed = padded_2(volume, (("space", 1), ("chan", 2)), 1)
    padded = jnp.pad(rimmed, ((0, 0), (0, 0), (0, 0), (1, 1)))
    pre_first = convolve(padded, weight_first, planes, rows, depth)
    pooled = pool_mean(jax.nn.silu(pre_first)).astype(jnp.bfloat16)
    whole = lax.all_gather(pooled, "chan", axis=2, tiled=True)
    framed = padded_2(whole, (("space", 1),), 1)
    deep_in = jnp.pad(framed, ((0, 0), (0, 0), (1, 1), (1, 1)))
    deep_planes = pooled.shape[1]
    deep_rows, deep_depth = framed.shape[2:]
    pre_deep = convolve(deep_in, weight_deep, deep_planes, deep_rows, deep_depth)
    deep_out = jax.nn.silu(pre_deep).astype(jnp.bfloat16).reshape(cotangent.shape)
    sigma = jax.nn.sigmoid(pre_deep)
    cot_grid = cotangent.reshape(pre_deep.shape).astype(jnp.float32)
    grad_pre = (cot_grid * sigma * (1.0 + pre_deep * (1.0 - sigma))).astype(jnp.bfloat16)
    local_grad = weight_terms(grad_pre, deep_in, deep_planes, deep_rows, deep_depth)
    return deep_out, lax.psum(local_grad, "space")


DN = (((1,), (0,)), ((), ()))
NT = (((1,), (1,)), ((), ()))
TN = (((0,), (0,)), ((), ()))


def place():
    role = lax.axis_index("space") ^ 1
    return lax.axis_index("chan"), role & 1, (role > 0) & (role < lax.axis_size("space") - 1)


def fill_patches(grid, moved, patches):
    planes, rows, cin, depth = grid.shape
    lane = lax.broadcasted_iota(jnp.int32, (rows * cin, depth), 1)
    for plane in range(planes):
        flat = grid[plane].reshape(rows * cin, depth).astype(jnp.float32)
        left = jnp.where(lane == 0, 0.0, pltpu.roll(flat, 1, 1))
        right = jnp.where(lane == depth - 1, 0.0, pltpu.roll(flat, depth - 1, 1))
        moved[0, plane] = left.astype(jnp.bfloat16).reshape(rows, cin, depth)
        moved[1, plane] = right.astype(jnp.bfloat16).reshape(rows, cin, depth)
    for plane in range(planes):
        for b in range(3):
            for c in range(3):
                at = ((plane * 3 + b) * 3 + c) * cin
                for row in range(rows - 2):
                    block = grid[plane, row + b] if c == 1 else moved[c // 2, plane, row + b]
                    patches[at : at + cin, row * depth : (row + 1) * depth] = block


def place_rows(grid, plane, owner, rows):
    rows = jnp.swapaxes(rows, 0, 1)
    for row in range(rows.shape[0]):
        grid[plane, 1 + owner * rows.shape[0] + row] = rows[row]


def silu(value):
    return value / (1.0 + jnp.exp(-value))


def first_part(chans, w_ref, near_ref, *refs):
    blocks, (part_ref, sums_ref, grid, moved, patches) = refs[:chans], refs[-5:]
    planes, rows, cin, depth = grid.shape
    mine, odd, _ = place()
    edge = jnp.zeros((cin, depth), jnp.bfloat16)
    for plane in range(planes):
        grid[plane, 0] = edge
        grid[plane, rows - 1] = edge
    for k in range(chans):
        place_rows(grid, 0, mine ^ k, blocks[k][:, odd])
        place_rows(grid, 1, mine ^ k, blocks[k][:, 1 - odd])
        place_rows(grid, 2, mine ^ k, near_ref[chans - 1 - k])
    fill_patches(grid, moved, patches)
    to_far, centre, from_far = w_ref[2 * odd], w_ref[1], w_ref[2 - 2 * odd]
    inner = jnp.concatenate([to_far, centre, from_far], axis=0)
    outer = jnp.concatenate([centre, from_far], axis=0)
    for pair in range((rows - 2) // 2):
        cols = slice(pair * 2 * depth, (pair + 1) * 2 * depth)
        act = silu(lax.dot_general(inner, patches[:, cols], TN, preferred_element_type=jnp.float32))
        sums_ref[:, pair * depth : (pair + 1) * depth] = act[:, :depth] + act[:, depth:]
        part_ref[:, cols] = lax.dot_general(
            outer, patches[: outer.shape[0], cols], TN, preferred_element_type=jnp.float32
        )


def first_rest(w_ref, far_ref, part_ref, sums_ref, *refs):
    out_ref, grid, moved, patches = refs[-4:]
    _, rows, cin, depth = grid.shape
    mine, odd, has_far = place()
    edge = jnp.zeros((cin, depth), jnp.bfloat16)
    grid[0, 0] = edge
    grid[0, rows - 1] = edge
    for k in range(far_ref.shape[0]):
        rows_k = far_ref[far_ref.shape[0] - 1 - k]
        place_rows(grid, 0, mine ^ k, jnp.where(has_far, rows_k, jnp.zeros_like(rows_k)))
    fill_patches(grid, moved, patches)
    to_far = w_ref[2 * odd]
    sums = []
    for pair in range((rows - 2) // 2):
        cols = slice(pair * 2 * depth, (pair + 1) * 2 * depth)
        term = lax.dot_general(to_far, patches[:, cols], TN, preferred_element_type=jnp.float32)
        act = silu(part_ref[:, cols] + term)
        total = sums_ref[:, pair * depth : (pair + 1) * depth] + act[:, :depth] + act[:, depth:]
        sums.append(total * 0.125)
    fold_in = lax.broadcasted_iota(jnp.int32, (2 * depth, depth), 0)
    fold_out = lax.broadcasted_iota(jnp.int32, (2 * depth, depth), 1)
    fold = (fold_in // 2 == fold_out).astype(jnp.float32)
    for pair in range(0, len(sums), 2):
        both = jnp.concatenate([sums[pair], sums[pair + 1]], axis=1)
        halved = lax.dot_general(
            both, fold, DN, precision=lax.Precision.HIGHEST, preferred_element_type=jnp.float32
        )
        out_ref[:, pair // 2 * depth : (pair // 2 + 1) * depth] = halved.astype(jnp.bfloat16)


def deep_kernel(rowlen, order, w_ref, cot_ref, cot_swapped_ref, *refs):
    count = len(refs) - 7
    planes, refs = refs[:count], refs[count:]
    out_ref, grad_ref, held, cot, act, taps, shifted = refs
    cmid, cells = held.shape[1:]
    cout = cot.shape[1]
    mine = lax.axis_index("space")
    for k in range(count):
        held[mine ^ 1 ^ k] = planes[k][...]
    for k, bits in enumerate(order):
        cot[mine ^ bits] = cot_ref[k]
        cot[mine ^ bits ^ 1] = cot_swapped_ref[k]
    lane = lax.broadcasted_iota(jnp.int32, (cmid, cells), 1)
    z = lane % rowlen
    edge = jnp.zeros((9 * cmid, cells), jnp.bfloat16)
    taps[:, :cells] = edge
    taps[:, (count + 1) * cells :] = edge
    for slot in range(count):
        plane = held[slot].astype(jnp.float32)
        for b in range(3):
            for c in range(3):
                shift = (b - 1) * rowlen + (c - 1)
                value = plane
                if shift:
                    value = pltpu.roll(plane, (-shift) % cells, 1)
                    ok = None
                    if b == 0:
                        ok = lane >= rowlen
                    if b == 2:
                        ok = lane < cells - rowlen
                    if c != 1:
                        inside = z > 0 if c == 0 else z < rowlen - 1
                        ok = inside if ok is None else ok & inside
                    value = jnp.where(ok, value, 0.0)
                row = (b * 3 + c) * cmid
                taps[row : row + cmid, (slot + 1) * cells : (slot + 2) * cells] = value.astype(jnp.bfloat16)
    depth = 9 * cmid
    empty = jnp.zeros((cout, cells), jnp.bfloat16)
    for p in range(count):
        rhs = jnp.concatenate(
            [taps[:, (p + a) * cells : (p + a + 1) * cells] for a in range(3)], axis=0
        )
        value = lax.dot_general(w_ref[...], rhs, DN, preferred_element_type=jnp.float32)
        sigma = 1.0 / (1.0 + jnp.exp(-value))
        act[p] = (value * sigma).astype(jnp.bfloat16)
        grad_pre = cot[p].astype(jnp.float32) * sigma * (1.0 + value * (1.0 - sigma))
        for a in range(3):
            q = p + a - 1
            if 0 <= q < count:
                shifted[a * cout : (a + 1) * cout, q * cells : (q + 1) * cells] = grad_pre.astype(
                    jnp.bfloat16
                )
    shifted[:cout, (count - 1) * cells :] = empty
    shifted[2 * cout :, :cells] = empty
    out_ref[...] = act[mine]
    half = depth // 2
    for row in range(0, depth, half):
        terms = lax.dot_general(
            taps[row : row + half, cells : (count + 1) * cells],
            shifted[...],
            NT,
            preferred_element_type=jnp.float32,
        )
        for a in range(3):
            at = a * depth + row
            grad_ref[at : at + half] = terms[:, a * cout : (a + 1) * cout]


def after(event, *arrays):
    return lax.optimization_barrier((event, *arrays))[1:]


def swap(array, axis, bits):
    peers = lax.axis_size(axis)
    return lax.ppermute(array, axis, [(i, i ^ bits) for i in range(peers)])


def crossed(array, bits):
    spaces, chans = lax.axis_size("space"), lax.axis_size("chan")
    pairs = [(s * chans + c, (s ^ 1) * chans + (c ^ bits)) for s in range(spaces) for c in range(chans)]
    return lax.ppermute(array, ("space", "chan"), pairs)


def spread(direct, order):
    pieces = {}
    for bits, piece in zip(order, direct):
        pieces[bits], pieces[bits ^ 1] = piece, swap(piece, "space", 1)
    return [pieces[k] for k in range(2 * len(order))]


def by_gather(volume, weight_first, weight_deep, cotangent):
    cin, planes, rows, depth = volume.shape
    spaces, chans = lax.axis_size("space"), lax.axis_size("chan")
    cmid, cout, cells = weight_first.shape[3], weight_deep.shape[3], cotangent.shape[2]
    all_rows = chans * rows
    odd = (lax.axis_index("space") ^ 1) & 1
    order = [0] + [k | 1 for k in range(2, spaces, 2)]
    vmem = pl.BlockSpec(memory_space=pltpu.VMEM)

    as_given = Layout(major_to_minor=(0, 1, 2, 3))
    blocks = [with_layout_constraint(crossed(volume, k), as_given) for k in range(chans)[::-1]][::-1]
    first = jnp.stack([piece[:, 0] for piece in blocks[::-1]])
    last = jnp.stack([piece[:, planes - 1] for piece in blocks[::-1]])
    near = swap(jnp.where(odd == 1, first, last), "space", 1)
    pairs = [(i ^ 1, ((i + 1) % spaces) ^ 1) for i in range(1, spaces, 2)]
    far = lax.ppermute(
        jnp.where(odd == 1, last, first), "space", pairs + [(j, i) for i, j in pairs]
    )

    cots = [cotangent[:, 0]]
    cots = cots + [swap(cots[0], "space", bits) for bits in order[1:]]

    taps_first = jnp.transpose(weight_first, (0, 1, 2, 4, 3)).reshape(3, 9 * cin, cmid)

    def patch_scratch(count):
        return [
            pltpu.VMEM((count, all_rows + 2, cin, depth), jnp.bfloat16),
            pltpu.VMEM((2, count, all_rows + 2, cin, depth), jnp.bfloat16),
            pltpu.VMEM((count * 9 * cin, all_rows * depth), jnp.bfloat16),
        ]

    params = pltpu.CompilerParams(vmem_limit_bytes=32 * 2**20)
    part, sums = pl.pallas_call(
        functools.partial(first_part, chans),
        out_shape=(
            jax.ShapeDtypeStruct((cmid, all_rows * depth), jnp.float32),
            jax.ShapeDtypeStruct((cmid, all_rows * depth // 2), jnp.float32),
        ),
        in_specs=[vmem] * (2 + chans) + [pl.BlockSpec(memory_space=pl.ANY)] * (len(order) - 1),
        out_specs=(vmem, vmem),
        scratch_shapes=patch_scratch(planes + 1),
        compiler_params=params,
        name="first_part",
        cost_estimate=pl.CostEstimate(flops=0, bytes_accessed=5000000, transcendentals=0),
    )(taps_first, near, *blocks, *cots[1:])

    pooled = pl.pallas_call(
        first_rest,
        out_shape=jax.ShapeDtypeStruct((cmid, cells), jnp.bfloat16),
        in_specs=[vmem] * 4,
        out_specs=vmem,
        scratch_shapes=patch_scratch(1),
        compiler_params=params,
        name="first_rest",
        cost_estimate=pl.CostEstimate(flops=0, bytes_accessed=4000000, transcendentals=0),
    )(taps_first, far, part, sums)

    direct = [pooled] + [swap(pooled, "space", bits) for bits in order[1:]]
    (weight_deep,) = after(pooled, weight_deep)
    taps_deep = jnp.transpose(weight_deep, (3, 0, 1, 2, 4)).reshape(cout, 27 * cmid)
    cots = after(pooled, *cots)
    cots = jnp.stack(cots)
    cots_swapped = swap(cots, "space", 1)
    all_pooled = spread(direct, order)

    deep_out, terms = pl.pallas_call(
        functools.partial(deep_kernel, depth // 2, order),
        out_shape=(
            jax.ShapeDtypeStruct((cout, cells), jnp.bfloat16),
            jax.ShapeDtypeStruct((27 * cmid, cout), jnp.float32),
        ),
        in_specs=[vmem] * (3 + spaces),
        out_specs=(vmem, vmem),
        scratch_shapes=[
            pltpu.VMEM((spaces, cmid, cells), jnp.bfloat16),
            pltpu.VMEM((spaces, cout, cells), jnp.bfloat16),
            pltpu.VMEM((spaces, cout, cells), jnp.bfloat16),
            pltpu.VMEM((9 * cmid, (spaces + 2) * cells), jnp.bfloat16),
            pltpu.VMEM((3 * cout, spaces * cells), jnp.bfloat16),
        ],
        compiler_params=params,
        name="deep",
        cost_estimate=pl.CostEstimate(flops=0, bytes_accessed=12000000, transcendentals=0),
    )(taps_deep, cots, cots_swapped, *all_pooled)

    grad = jnp.transpose(terms.reshape(3, 3, 3, cmid, cout), (0, 1, 2, 4, 3))
    return deep_out[:, None], grad


def on_device(volume, weight_first, weight_deep, cotangent):
    spaces, chans = lax.axis_size("space"), lax.axis_size("chan")
    powers = spaces & (spaces - 1) == 0 and chans & (chans - 1) == 0
    fits = spaces * cotangent.shape[0] * cotangent.shape[2] <= 2**20
    if powers and fits and spaces > 1 and volume.shape[1:3] == (2, 2):
        return by_gather(volume, weight_first, weight_deep, cotangent)
    return by_halos(volume, weight_first, weight_deep, cotangent)


def solution(mesh):
    return jax.shard_map(
        on_device,
        mesh=mesh,
        in_specs=(
            P(None, "space", "chan", None),
            P(),
            P(None, None, None, "chan", None),
            P("chan", "space", None),
        ),
        out_specs=(P("chan", "space", None), P(None, None, None, "chan", None)),
        check_vma=False,
    )
```

```python
import functools

import jax
import jax.numpy as jnp
from jax import lax
from jax.experimental import pallas as pl
from jax.experimental.layout import Layout, with_layout_constraint
from jax.experimental.pallas import tpu as pltpu
from jax.sharding import PartitionSpec as P


def padded_2(array, sides, width):
    for axis, dim in sides:
        peers, length = (lax.axis_size(axis), array.shape[dim])
        up = [(i, (i + 1) % peers) for i in range(peers - 1)]
        down = [(j, i) for i, j in up]
        last = lax.slice_in_dim(array, length - width, length, axis=dim)
        leading = lax.slice_in_dim(array, 0, width, axis=dim)
        before = lax.ppermute(last, axis, up)
        after = lax.ppermute(leading, axis, down)
        array = jnp.concatenate([before, array, after], axis=dim)
    return array


def windows(padded, planes, rows, depth):
    for offset_x in range(3):
        for offset_y in range(3):
            for offset_z in range(3):
                yield (offset_x, offset_y, offset_z), padded[
                    :,
                    offset_x : offset_x + planes,
                    offset_y : offset_y + rows,
                    offset_z : offset_z + depth,
                ]


def convolve(padded, weight, planes, rows, depth):
    total = jnp.zeros((weight.shape[3], planes, rows, depth), jnp.float32)
    for tap, window in windows(padded, planes, rows, depth):
        total = total + jnp.einsum(
            "oc,cxyz->oxyz", weight[tap], window, preferred_element_type=jnp.float32
        )
    return total


def weight_terms(grad_pre, padded, planes, rows, depth):
    terms = [
        jnp.einsum("oxyz,cxyz->oc", grad_pre, window, preferred_element_type=jnp.float32)
        for _, window in windows(padded, planes, rows, depth)
    ]
    return jnp.stack(terms).reshape((3, 3, 3) + terms[0].shape)


def pool_mean(act):
    chans, planes, rows, depth = act.shape
    blocks = act.reshape(chans, planes // 2, 2, rows // 2, 2, depth // 2, 2)
    return jnp.mean(blocks, axis=(2, 4, 6))


def by_halos(volume, weight_first, weight_deep, cotangent):
    planes, rows, depth = volume.shape[1:]
    rimmed = padded_2(volume, (("space", 1), ("chan", 2)), 1)
    padded = jnp.pad(rimmed, ((0, 0), (0, 0), (0, 0), (1, 1)))
    pre_first = convolve(padded, weight_first, planes, rows, depth)
    pooled = pool_mean(jax.nn.silu(pre_first)).astype(jnp.bfloat16)
    whole = lax.all_gather(pooled, "chan", axis=2, tiled=True)
    framed = padded_2(whole, (("space", 1),), 1)
    deep_in = jnp.pad(framed, ((0, 0), (0, 0), (1, 1), (1, 1)))
    deep_planes = pooled.shape[1]
    deep_rows, deep_depth = framed.shape[2:]
    pre_deep = convolve(deep_in, weight_deep, deep_planes, deep_rows, deep_depth)
    deep_out = jax.nn.silu(pre_deep).astype(jnp.bfloat16).reshape(cotangent.shape)
    sigma = jax.nn.sigmoid(pre_deep)
    cot_grid = cotangent.reshape(pre_deep.shape).astype(jnp.float32)
    grad_pre = (cot_grid * sigma * (1.0 + pre_deep * (1.0 - sigma))).astype(jnp.bfloat16)
    local_grad = weight_terms(grad_pre, deep_in, deep_planes, deep_rows, deep_depth)
    return deep_out, lax.psum(local_grad, "space")


DN = (((1,), (0,)), ((), ()))
NT = (((1,), (1,)), ((), ()))
TN = (((0,), (0,)), ((), ()))


def place():
    role = lax.axis_index("space") ^ 1
    return lax.axis_index("chan"), role & 1, (role > 0) & (role < lax.axis_size("space") - 1)


def fill_patches(grid, moved, patches):
    planes, rows, cin, depth = grid.shape
    lane = lax.broadcasted_iota(jnp.int32, (rows * cin, depth), 1)
    for plane in range(planes):
        flat = grid[plane].reshape(rows * cin, depth).astype(jnp.float32)
        left = jnp.where(lane == 0, 0.0, pltpu.roll(flat, 1, 1))
        right = jnp.where(lane == depth - 1, 0.0, pltpu.roll(flat, depth - 1, 1))
        moved[0, plane] = left.astype(jnp.bfloat16).reshape(rows, cin, depth)
        moved[1, plane] = right.astype(jnp.bfloat16).reshape(rows, cin, depth)
    for plane in range(planes):
        for b in range(3):
            for c in range(3):
                at = ((plane * 3 + b) * 3 + c) * cin
                for row in range(rows - 2):
                    block = grid[plane, row + b] if c == 1 else moved[c // 2, plane, row + b]
                    patches[at : at + cin, row * depth : (row + 1) * depth] = block


def place_rows(grid, plane, owner, rows):
    rows = jnp.swapaxes(rows, 0, 1)
    for row in range(rows.shape[0]):
        grid[plane, 1 + owner * rows.shape[0] + row] = rows[row]


def silu(value):
    return value / (1.0 + jnp.exp(-value))


def first_part(chans, w_ref, near_ref, *refs):
    blocks, (part_ref, sums_ref, grid, moved, patches) = refs[:chans], refs[-5:]
    planes, rows, cin, depth = grid.shape
    mine, odd, _ = place()
    edge = jnp.zeros((cin, depth), jnp.bfloat16)
    for plane in range(planes):
        grid[plane, 0] = edge
        grid[plane, rows - 1] = edge
    for k in range(chans):
        place_rows(grid, 0, mine ^ k, blocks[k][:, odd])
        place_rows(grid, 1, mine ^ k, blocks[k][:, 1 - odd])
        place_rows(grid, 2, mine ^ k, near_ref[chans - 1 - k])
    fill_patches(grid, moved, patches)
    to_far, centre, from_far = w_ref[2 * odd], w_ref[1], w_ref[2 - 2 * odd]
    inner = jnp.concatenate([to_far, centre, from_far], axis=0)
    outer = jnp.concatenate([centre, from_far], axis=0)
    for pair in range((rows - 2) // 2):
        cols = slice(pair * 2 * depth, (pair + 1) * 2 * depth)
        act = silu(lax.dot_general(inner, patches[:, cols], TN, preferred_element_type=jnp.float32))
        sums_ref[:, pair * depth : (pair + 1) * depth] = act[:, :depth] + act[:, depth:]
        part_ref[:, cols] = lax.dot_general(
            outer, patches[: outer.shape[0], cols], TN, preferred_element_type=jnp.float32
        )


def first_rest(w_ref, far_ref, part_ref, sums_ref, *refs):
    out_ref, grid, moved, patches = refs[-4:]
    _, rows, cin, depth = grid.shape
    mine, odd, has_far = place()
    edge = jnp.zeros((cin, depth), jnp.bfloat16)
    grid[0, 0] = edge
    grid[0, rows - 1] = edge
    for k in range(far_ref.shape[0]):
        rows_k = far_ref[far_ref.shape[0] - 1 - k]
        place_rows(grid, 0, mine ^ k, jnp.where(has_far, rows_k, jnp.zeros_like(rows_k)))
    fill_patches(grid, moved, patches)
    terms = lax.dot_general(w_ref[2 * odd], patches[...], TN, preferred_element_type=jnp.float32)
    sums = []
    for pair in range((rows - 2) // 2):
        cols = slice(pair * 2 * depth, (pair + 1) * 2 * depth)
        act = silu(part_ref[:, cols] + terms[:, cols])
        total = sums_ref[:, pair * depth : (pair + 1) * depth] + act[:, :depth] + act[:, depth:]
        sums.append(total * 0.125)
    fold_in = lax.broadcasted_iota(jnp.int32, (2 * depth, depth), 0)
    fold_out = lax.broadcasted_iota(jnp.int32, (2 * depth, depth), 1)
    fold = (fold_in // 2 == fold_out).astype(jnp.float32)
    for pair in range(0, len(sums), 2):
        both = jnp.concatenate([sums[pair], sums[pair + 1]], axis=1)
        halved = lax.dot_general(
            both, fold, DN, precision=lax.Precision.HIGHEST, preferred_element_type=jnp.float32
        )
        out_ref[:, pair // 2 * depth : (pair // 2 + 1) * depth] = halved.astype(jnp.bfloat16)


def deep_kernel(rowlen, order, w_ref, cot_ref, cot_swapped_ref, *refs):
    count = len(refs) - 7
    planes, refs = refs[:count], refs[count:]
    out_ref, grad_ref, held, cot, act, taps, shifted = refs
    cmid, cells = held.shape[1:]
    cout = cot.shape[1]
    mine = lax.axis_index("space")
    for k in range(count):
        held[mine ^ 1 ^ k] = planes[k][...]
    for k, bits in enumerate(order):
        cot[mine ^ bits] = cot_ref[k]
        cot[mine ^ bits ^ 1] = cot_swapped_ref[k]
    lane = lax.broadcasted_iota(jnp.int32, (cmid, cells), 1)
    z = lane % rowlen
    edge = jnp.zeros((9 * cmid, cells), jnp.bfloat16)
    taps[:, :cells] = edge
    taps[:, (count + 1) * cells :] = edge
    for slot in range(count):
        plane = held[slot].astype(jnp.float32)
        for b in range(3):
            for c in range(3):
                shift = (b - 1) * rowlen + (c - 1)
                value = plane
                if shift:
                    value = pltpu.roll(plane, (-shift) % cells, 1)
                    ok = None
                    if b == 0:
                        ok = lane >= rowlen
                    if b == 2:
                        ok = lane < cells - rowlen
                    if c != 1:
                        inside = z > 0 if c == 0 else z < rowlen - 1
                        ok = inside if ok is None else ok & inside
                    value = jnp.where(ok, value, 0.0)
                row = (b * 3 + c) * cmid
                taps[row : row + cmid, (slot + 1) * cells : (slot + 2) * cells] = value.astype(jnp.bfloat16)
    depth = 9 * cmid
    empty = jnp.zeros((cout, cells), jnp.bfloat16)
    for p in range(count):
        rhs = jnp.concatenate(
            [taps[:, (p + a) * cells : (p + a + 1) * cells] for a in range(3)], axis=0
        )
        value = lax.dot_general(w_ref[...], rhs, DN, preferred_element_type=jnp.float32)
        sigma = 1.0 / (1.0 + jnp.exp(-value))
        act[p] = (value * sigma).astype(jnp.bfloat16)
        grad_pre = cot[p].astype(jnp.float32) * sigma * (1.0 + value * (1.0 - sigma))
        for a in range(3):
            q = p + a - 1
            if 0 <= q < count:
                shifted[a * cout : (a + 1) * cout, q * cells : (q + 1) * cells] = grad_pre.astype(
                    jnp.bfloat16
                )
    shifted[:cout, (count - 1) * cells :] = empty
    shifted[2 * cout :, :cells] = empty
    out_ref[...] = act[mine]
    half = depth // 2
    for row in range(0, depth, half):
        terms = lax.dot_general(
            taps[row : row + half, cells : (count + 1) * cells],
            shifted[...],
            NT,
            preferred_element_type=jnp.float32,
        )
        for a in range(3):
            at = a * depth + row
            grad_ref[at : at + half] = terms[:, a * cout : (a + 1) * cout]


def after(event, *arrays):
    return lax.optimization_barrier((event, *arrays))[1:]


def swap(array, axis, bits):
    peers = lax.axis_size(axis)
    return lax.ppermute(array, axis, [(i, i ^ bits) for i in range(peers)])


def crossed(array, bits):
    spaces, chans = lax.axis_size("space"), lax.axis_size("chan")
    pairs = [(s * chans + c, (s ^ 1) * chans + (c ^ bits)) for s in range(spaces) for c in range(chans)]
    return lax.ppermute(array, ("space", "chan"), pairs)


def spread(direct, order):
    pieces = {}
    for bits, piece in zip(order, direct):
        pieces[bits], pieces[bits ^ 1] = piece, swap(piece, "space", 1)
    return [pieces[k] for k in range(2 * len(order))]


def by_gather(volume, weight_first, weight_deep, cotangent):
    cin, planes, rows, depth = volume.shape
    spaces, chans = lax.axis_size("space"), lax.axis_size("chan")
    cmid, cout, cells = weight_first.shape[3], weight_deep.shape[3], cotangent.shape[2]
    all_rows = chans * rows
    odd = (lax.axis_index("space") ^ 1) & 1
    order = [0] + [k | 1 for k in range(2, spaces, 2)]
    vmem = pl.BlockSpec(memory_space=pltpu.VMEM)

    as_given = Layout(major_to_minor=(0, 1, 2, 3))
    blocks = [with_layout_constraint(crossed(volume, k), as_given) for k in range(chans)[::-1]][::-1]
    first = jnp.stack([piece[:, 0] for piece in blocks[::-1]])
    last = jnp.stack([piece[:, planes - 1] for piece in blocks[::-1]])
    near = swap(jnp.where(odd == 1, first, last), "space", 1)
    pairs = [(i ^ 1, ((i + 1) % spaces) ^ 1) for i in range(1, spaces, 2)]
    far = lax.ppermute(
        jnp.where(odd == 1, last, first), "space", pairs + [(j, i) for i, j in pairs]
    )

    cots = [cotangent[:, 0]]
    cots = cots + [swap(cots[0], "space", bits) for bits in order[1:]]

    taps_first = jnp.transpose(weight_first, (0, 1, 2, 4, 3)).reshape(3, 9 * cin, cmid)

    def patch_scratch(count):
        return [
            pltpu.VMEM((count, all_rows + 2, cin, depth), jnp.bfloat16),
            pltpu.VMEM((2, count, all_rows + 2, cin, depth), jnp.bfloat16),
            pltpu.VMEM((count * 9 * cin, all_rows * depth), jnp.bfloat16),
        ]

    params = pltpu.CompilerParams(vmem_limit_bytes=32 * 2**20)
    part, sums = pl.pallas_call(
        functools.partial(first_part, chans),
        out_shape=(
            jax.ShapeDtypeStruct((cmid, all_rows * depth), jnp.float32),
            jax.ShapeDtypeStruct((cmid, all_rows * depth // 2), jnp.float32),
        ),
        in_specs=[vmem] * (2 + chans) + [pl.BlockSpec(memory_space=pl.ANY)] * (len(order) - 1),
        out_specs=(vmem, vmem),
        scratch_shapes=patch_scratch(planes + 1),
        compiler_params=params,
        name="first_part",
        cost_estimate=pl.CostEstimate(flops=0, bytes_accessed=5000000, transcendentals=0),
    )(taps_first, near, *blocks, *cots[1:])

    pooled = pl.pallas_call(
        first_rest,
        out_shape=jax.ShapeDtypeStruct((cmid, cells), jnp.bfloat16),
        in_specs=[vmem] * 4,
        out_specs=vmem,
        scratch_shapes=patch_scratch(1),
        compiler_params=params,
        name="first_rest",
        cost_estimate=pl.CostEstimate(flops=0, bytes_accessed=4000000, transcendentals=0),
    )(taps_first, far, part, sums)

    direct = [pooled] + [swap(pooled, "space", bits) for bits in order[1:]]
    (weight_deep,) = after(pooled, weight_deep)
    taps_deep = jnp.transpose(weight_deep, (3, 0, 1, 2, 4)).reshape(cout, 27 * cmid)
    cots = after(pooled, *cots)
    cots = jnp.stack(cots)
    cots_swapped = swap(cots, "space", 1)
    all_pooled = spread(direct, order)

    deep_out, terms = pl.pallas_call(
        functools.partial(deep_kernel, depth // 2, order),
        out_shape=(
            jax.ShapeDtypeStruct((cout, cells), jnp.bfloat16),
            jax.ShapeDtypeStruct((27 * cmid, cout), jnp.float32),
        ),
        in_specs=[vmem] * (3 + spaces),
        out_specs=(vmem, vmem),
        scratch_shapes=[
            pltpu.VMEM((spaces, cmid, cells), jnp.bfloat16),
            pltpu.VMEM((spaces, cout, cells), jnp.bfloat16),
            pltpu.VMEM((spaces, cout, cells), jnp.bfloat16),
            pltpu.VMEM((9 * cmid, (spaces + 2) * cells), jnp.bfloat16),
            pltpu.VMEM((3 * cout, spaces * cells), jnp.bfloat16),
        ],
        compiler_params=params,
        name="deep",
        cost_estimate=pl.CostEstimate(flops=0, bytes_accessed=12000000, transcendentals=0),
    )(taps_deep, cots, cots_swapped, *all_pooled)

    grad = jnp.transpose(terms.reshape(3, 3, 3, cmid, cout), (0, 1, 2, 4, 3))
    return deep_out[:, None], grad


def on_device(volume, weight_first, weight_deep, cotangent):
    spaces, chans = lax.axis_size("space"), lax.axis_size("chan")
    powers = spaces & (spaces - 1) == 0 and chans & (chans - 1) == 0
    fits = spaces * cotangent.shape[0] * cotangent.shape[2] <= 2**20
    if powers and fits and spaces > 1 and volume.shape[1:3] == (2, 2):
        return by_gather(volume, weight_first, weight_deep, cotangent)
    return by_halos(volume, weight_first, weight_deep, cotangent)


def solution(mesh):
    return jax.shard_map(
        on_device,
        mesh=mesh,
        in_specs=(
            P(None, "space", "chan", None),
            P(),
            P(None, None, None, "chan", None),
            P("chan", "space", None),
        ),
        out_specs=(P("chan", "space", None), P(None, None, None, "chan", None)),
        check_vma=False,
    )
```

```python
import functools

import jax
import jax.numpy as jnp
from jax import lax
from jax.experimental import pallas as pl
from jax.experimental.layout import Layout, with_layout_constraint
from jax.experimental.pallas import tpu as pltpu
from jax.sharding import PartitionSpec as P


def padded_2(array, sides, width):
    for axis, dim in sides:
        peers, length = (lax.axis_size(axis), array.shape[dim])
        up = [(i, (i + 1) % peers) for i in range(peers - 1)]
        down = [(j, i) for i, j in up]
        last = lax.slice_in_dim(array, length - width, length, axis=dim)
        leading = lax.slice_in_dim(array, 0, width, axis=dim)
        before = lax.ppermute(last, axis, up)
        after = lax.ppermute(leading, axis, down)
        array = jnp.concatenate([before, array, after], axis=dim)
    return array


def windows(padded, planes, rows, depth):
    for offset_x in range(3):
        for offset_y in range(3):
            for offset_z in range(3):
                yield (offset_x, offset_y, offset_z), padded[
                    :,
                    offset_x : offset_x + planes,
                    offset_y : offset_y + rows,
                    offset_z : offset_z + depth,
                ]


def convolve(padded, weight, planes, rows, depth):
    total = jnp.zeros((weight.shape[3], planes, rows, depth), jnp.float32)
    for tap, window in windows(padded, planes, rows, depth):
        total = total + jnp.einsum(
            "oc,cxyz->oxyz", weight[tap], window, preferred_element_type=jnp.float32
        )
    return total


def weight_terms(grad_pre, padded, planes, rows, depth):
    terms = [
        jnp.einsum("oxyz,cxyz->oc", grad_pre, window, preferred_element_type=jnp.float32)
        for _, window in windows(padded, planes, rows, depth)
    ]
    return jnp.stack(terms).reshape((3, 3, 3) + terms[0].shape)


def pool_mean(act):
    chans, planes, rows, depth = act.shape
    blocks = act.reshape(chans, planes // 2, 2, rows // 2, 2, depth // 2, 2)
    return jnp.mean(blocks, axis=(2, 4, 6))


def by_halos(volume, weight_first, weight_deep, cotangent):
    planes, rows, depth = volume.shape[1:]
    rimmed = padded_2(volume, (("space", 1), ("chan", 2)), 1)
    padded = jnp.pad(rimmed, ((0, 0), (0, 0), (0, 0), (1, 1)))
    pre_first = convolve(padded, weight_first, planes, rows, depth)
    pooled = pool_mean(jax.nn.silu(pre_first)).astype(jnp.bfloat16)
    whole = lax.all_gather(pooled, "chan", axis=2, tiled=True)
    framed = padded_2(whole, (("space", 1),), 1)
    deep_in = jnp.pad(framed, ((0, 0), (0, 0), (1, 1), (1, 1)))
    deep_planes = pooled.shape[1]
    deep_rows, deep_depth = framed.shape[2:]
    pre_deep = convolve(deep_in, weight_deep, deep_planes, deep_rows, deep_depth)
    deep_out = jax.nn.silu(pre_deep).astype(jnp.bfloat16).reshape(cotangent.shape)
    sigma = jax.nn.sigmoid(pre_deep)
    cot_grid = cotangent.reshape(pre_deep.shape).astype(jnp.float32)
    grad_pre = (cot_grid * sigma * (1.0 + pre_deep * (1.0 - sigma))).astype(jnp.bfloat16)
    local_grad = weight_terms(grad_pre, deep_in, deep_planes, deep_rows, deep_depth)
    return deep_out, lax.psum(local_grad, "space")


DN = (((1,), (0,)), ((), ()))
NT = (((1,), (1,)), ((), ()))
TN = (((0,), (0,)), ((), ()))


def place():
    role = lax.axis_index("space") ^ 1
    return lax.axis_index("chan"), role & 1, (role > 0) & (role < lax.axis_size("space") - 1)


def fill_patches(grid, moved, patches):
    planes, rows, cin, depth = grid.shape
    lane = lax.broadcasted_iota(jnp.int32, (rows * cin, depth), 1)
    for plane in range(planes):
        flat = grid[plane].reshape(rows * cin, depth).astype(jnp.float32)
        left = jnp.where(lane == 0, 0.0, pltpu.roll(flat, 1, 1))
        right = jnp.where(lane == depth - 1, 0.0, pltpu.roll(flat, depth - 1, 1))
        moved[0, plane] = left.astype(jnp.bfloat16).reshape(rows, cin, depth)
        moved[1, plane] = right.astype(jnp.bfloat16).reshape(rows, cin, depth)
    for plane in range(planes):
        for b in range(3):
            for c in range(3):
                at = ((plane * 3 + b) * 3 + c) * cin
                for row in range(rows - 2):
                    block = grid[plane, row + b] if c == 1 else moved[c // 2, plane, row + b]
                    patches[at : at + cin, row * depth : (row + 1) * depth] = block


def place_rows(grid, plane, owner, rows):
    rows = jnp.swapaxes(rows, 0, 1)
    for row in range(rows.shape[0]):
        grid[plane, 1 + owner * rows.shape[0] + row] = rows[row]


def silu(value):
    return value / (1.0 + jnp.exp(-value))


def first_part(chans, w_ref, near_ref, *refs):
    blocks, (part_ref, sums_ref, grid, moved, patches) = refs[:chans], refs[-5:]
    planes, rows, cin, depth = grid.shape
    mine, odd, _ = place()
    edge = jnp.zeros((cin, depth), jnp.bfloat16)
    for plane in range(planes):
        grid[plane, 0] = edge
        grid[plane, rows - 1] = edge
    for k in range(chans):
        place_rows(grid, 0, mine ^ k, blocks[k][:, odd])
        place_rows(grid, 1, mine ^ k, blocks[k][:, 1 - odd])
        place_rows(grid, 2, mine ^ k, near_ref[chans - 1 - k])
    fill_patches(grid, moved, patches)
    to_far, centre, from_far = w_ref[2 * odd], w_ref[1], w_ref[2 - 2 * odd]
    inner = jnp.concatenate([to_far, centre, from_far], axis=0)
    outer = jnp.concatenate([centre, from_far], axis=0)
    for pair in range((rows - 2) // 2):
        cols = slice(pair * 2 * depth, (pair + 1) * 2 * depth)
        act = silu(lax.dot_general(inner, patches[:, cols], TN, preferred_element_type=jnp.float32))
        sums_ref[:, pair * depth : (pair + 1) * depth] = act[:, :depth] + act[:, depth:]
        part_ref[:, cols] = lax.dot_general(
            outer, patches[: outer.shape[0], cols], TN, preferred_element_type=jnp.float32
        )


def first_rest(w_ref, far_ref, part_ref, sums_ref, *refs):
    out_ref, grid, moved, patches = refs[-4:]
    _, rows, cin, depth = grid.shape
    mine, odd, has_far = place()
    edge = jnp.zeros((cin, depth), jnp.bfloat16)
    grid[0, 0] = edge
    grid[0, rows - 1] = edge
    for k in range(far_ref.shape[0]):
        rows_k = far_ref[far_ref.shape[0] - 1 - k]
        place_rows(grid, 0, mine ^ k, jnp.where(has_far, rows_k, jnp.zeros_like(rows_k)))
    fill_patches(grid, moved, patches)
    to_far = w_ref[2 * odd]
    sums = []
    for pair in range((rows - 2) // 2):
        cols = slice(pair * 2 * depth, (pair + 1) * 2 * depth)
        term = lax.dot_general(to_far, patches[:, cols], TN, preferred_element_type=jnp.float32)
        act = silu(part_ref[:, cols] + term)
        total = sums_ref[:, pair * depth : (pair + 1) * depth] + act[:, :depth] + act[:, depth:]
        sums.append(total * 0.125)
    fold_in = lax.broadcasted_iota(jnp.int32, (2 * depth, depth), 0)
    fold_out = lax.broadcasted_iota(jnp.int32, (2 * depth, depth), 1)
    fold = (fold_in // 2 == fold_out).astype(jnp.float32)
    for pair in range(0, len(sums), 2):
        both = jnp.concatenate([sums[pair], sums[pair + 1]], axis=1)
        halved = lax.dot_general(
            both, fold, DN, precision=lax.Precision.HIGHEST, preferred_element_type=jnp.float32
        )
        out_ref[:, pair // 2 * depth : (pair // 2 + 1) * depth] = halved.astype(jnp.bfloat16)


def deep_kernel(rowlen, order, w_ref, cot_ref, cot_swapped_ref, *refs):
    count = len(refs) - 7
    planes, refs = refs[:count], refs[count:]
    out_ref, grad_ref, held, cot, act, taps, shifted = refs
    cmid, cells = held.shape[1:]
    cout = cot.shape[1]
    mine = lax.axis_index("space")
    for k in range(count):
        held[mine ^ 1 ^ k] = planes[k][...]
    for k, bits in enumerate(order):
        cot[mine ^ bits] = cot_ref[k]
        cot[mine ^ bits ^ 1] = cot_swapped_ref[k]
    lane = lax.broadcasted_iota(jnp.int32, (cmid, cells), 1)
    z = lane % rowlen
    edge = jnp.zeros((9 * cmid, cells), jnp.bfloat16)
    taps[:, :cells] = edge
    taps[:, (count + 1) * cells :] = edge
    for slot in range(count):
        plane = held[slot].astype(jnp.float32)
        for b in range(3):
            for c in range(3):
                shift = (b - 1) * rowlen + (c - 1)
                value = plane
                if shift:
                    value = pltpu.roll(plane, (-shift) % cells, 1)
                    ok = None
                    if b == 0:
                        ok = lane >= rowlen
                    if b == 2:
                        ok = lane < cells - rowlen
                    if c != 1:
                        inside = z > 0 if c == 0 else z < rowlen - 1
                        ok = inside if ok is None else ok & inside
                    value = jnp.where(ok, value, 0.0)
                row = (b * 3 + c) * cmid
                taps[row : row + cmid, (slot + 1) * cells : (slot + 2) * cells] = value.astype(jnp.bfloat16)
    depth = 9 * cmid
    empty = jnp.zeros((cout, cells), jnp.bfloat16)
    for p in range(count):
        rhs = jnp.concatenate(
            [taps[:, (p + a) * cells : (p + a + 1) * cells] for a in range(3)], axis=0
        )
        value = lax.dot_general(w_ref[...], rhs, DN, preferred_element_type=jnp.float32)
        sigma = 1.0 / (1.0 + jnp.exp(-value))
        out = value * sigma
        act[p] = out.astype(jnp.bfloat16)
        grad_pre = cot[p].astype(jnp.float32) * (sigma + out * (1.0 - sigma))
        for a in range(3):
            q = p + a - 1
            if 0 <= q < count:
                shifted[a * cout : (a + 1) * cout, q * cells : (q + 1) * cells] = grad_pre.astype(
                    jnp.bfloat16
                )
    shifted[:cout, (count - 1) * cells :] = empty
    shifted[2 * cout :, :cells] = empty
    out_ref[...] = act[mine]
    half = depth // 2
    for row in range(0, depth, half):
        terms = lax.dot_general(
            taps[row : row + half, cells : (count + 1) * cells],
            shifted[...],
            NT,
            preferred_element_type=jnp.float32,
        )
        for a in range(3):
            at = a * depth + row
            grad_ref[at : at + half] = terms[:, a * cout : (a + 1) * cout]


def after(event, *arrays):
    return lax.optimization_barrier((event, *arrays))[1:]


def swap(array, axis, bits):
    peers = lax.axis_size(axis)
    return lax.ppermute(array, axis, [(i, i ^ bits) for i in range(peers)])


def crossed(array, bits):
    spaces, chans = lax.axis_size("space"), lax.axis_size("chan")
    pairs = [(s * chans + c, (s ^ 1) * chans + (c ^ bits)) for s in range(spaces) for c in range(chans)]
    return lax.ppermute(array, ("space", "chan"), pairs)


def spread(direct, order):
    pieces = {}
    for bits, piece in zip(order, direct):
        pieces[bits], pieces[bits ^ 1] = piece, swap(piece, "space", 1)
    return [pieces[k] for k in range(2 * len(order))]


def by_gather(volume, weight_first, weight_deep, cotangent):
    cin, planes, rows, depth = volume.shape
    spaces, chans = lax.axis_size("space"), lax.axis_size("chan")
    cmid, cout, cells = weight_first.shape[3], weight_deep.shape[3], cotangent.shape[2]
    all_rows = chans * rows
    odd = (lax.axis_index("space") ^ 1) & 1
    order = [0] + [k | 1 for k in range(2, spaces, 2)]
    vmem = pl.BlockSpec(memory_space=pltpu.VMEM)

    as_given = Layout(major_to_minor=(0, 1, 2, 3))
    blocks = [with_layout_constraint(crossed(volume, k), as_given) for k in range(chans)[::-1]][::-1]
    first = jnp.stack([piece[:, 0] for piece in blocks[::-1]])
    last = jnp.stack([piece[:, planes - 1] for piece in blocks[::-1]])
    near = swap(jnp.where(odd == 1, first, last), "space", 1)
    pairs = [(i ^ 1, ((i + 1) % spaces) ^ 1) for i in range(1, spaces, 2)]
    far = lax.ppermute(
        jnp.where(odd == 1, last, first), "space", pairs + [(j, i) for i, j in pairs]
    )

    cots = [cotangent[:, 0]]
    cots = cots + [swap(cots[0], "space", bits) for bits in order[1:]]

    taps_first = jnp.transpose(weight_first, (0, 1, 2, 4, 3)).reshape(3, 9 * cin, cmid)

    def patch_scratch(count):
        return [
            pltpu.VMEM((count, all_rows + 2, cin, depth), jnp.bfloat16),
            pltpu.VMEM((2, count, all_rows + 2, cin, depth), jnp.bfloat16),
            pltpu.VMEM((count * 9 * cin, all_rows * depth), jnp.bfloat16),
        ]

    params = pltpu.CompilerParams(vmem_limit_bytes=32 * 2**20)
    part, sums = pl.pallas_call(
        functools.partial(first_part, chans),
        out_shape=(
            jax.ShapeDtypeStruct((cmid, all_rows * depth), jnp.float32),
            jax.ShapeDtypeStruct((cmid, all_rows * depth // 2), jnp.float32),
        ),
        in_specs=[vmem] * (2 + chans) + [pl.BlockSpec(memory_space=pl.ANY)] * (len(order) - 1),
        out_specs=(vmem, vmem),
        scratch_shapes=patch_scratch(planes + 1),
        compiler_params=params,
        name="first_part",
        cost_estimate=pl.CostEstimate(flops=0, bytes_accessed=5000000, transcendentals=0),
    )(taps_first, near, *blocks, *cots[1:])

    pooled = pl.pallas_call(
        first_rest,
        out_shape=jax.ShapeDtypeStruct((cmid, cells), jnp.bfloat16),
        in_specs=[vmem] * 4,
        out_specs=vmem,
        scratch_shapes=patch_scratch(1),
        compiler_params=params,
        name="first_rest",
        cost_estimate=pl.CostEstimate(flops=0, bytes_accessed=4000000, transcendentals=0),
    )(taps_first, far, part, sums)

    direct = [pooled] + [swap(pooled, "space", bits) for bits in order[1:]]
    (weight_deep,) = after(pooled, weight_deep)
    taps_deep = jnp.transpose(weight_deep, (3, 0, 1, 2, 4)).reshape(cout, 27 * cmid)
    cots = after(pooled, *cots)
    cots = jnp.stack(cots)
    cots_swapped = swap(cots, "space", 1)
    all_pooled = spread(direct, order)

    deep_out, terms = pl.pallas_call(
        functools.partial(deep_kernel, depth // 2, order),
        out_shape=(
            jax.ShapeDtypeStruct((cout, cells), jnp.bfloat16),
            jax.ShapeDtypeStruct((27 * cmid, cout), jnp.float32),
        ),
        in_specs=[vmem] * (3 + spaces),
        out_specs=(vmem, vmem),
        scratch_shapes=[
            pltpu.VMEM((spaces, cmid, cells), jnp.bfloat16),
            pltpu.VMEM((spaces, cout, cells), jnp.bfloat16),
            pltpu.VMEM((spaces, cout, cells), jnp.bfloat16),
            pltpu.VMEM((9 * cmid, (spaces + 2) * cells), jnp.bfloat16),
            pltpu.VMEM((3 * cout, spaces * cells), jnp.bfloat16),
        ],
        compiler_params=params,
        name="deep",
        cost_estimate=pl.CostEstimate(flops=0, bytes_accessed=12000000, transcendentals=0),
    )(taps_deep, cots, cots_swapped, *all_pooled)

    grad = jnp.transpose(terms.reshape(3, 3, 3, cmid, cout), (0, 1, 2, 4, 3))
    return deep_out[:, None], grad


def on_device(volume, weight_first, weight_deep, cotangent):
    spaces, chans = lax.axis_size("space"), lax.axis_size("chan")
    powers = spaces & (spaces - 1) == 0 and chans & (chans - 1) == 0
    fits = spaces * cotangent.shape[0] * cotangent.shape[2] <= 2**20
    if powers and fits and spaces > 1 and volume.shape[1:3] == (2, 2):
        return by_gather(volume, weight_first, weight_deep, cotangent)
    return by_halos(volume, weight_first, weight_deep, cotangent)


def solution(mesh):
    return jax.shard_map(
        on_device,
        mesh=mesh,
        in_specs=(
            P(None, "space", "chan", None),
            P(),
            P(None, None, None, "chan", None),
            P("chan", "space", None),
        ),
        out_specs=(P("chan", "space", None), P(None, None, None, "chan", None)),
        check_vma=False,
    )
```
